256 devices in a mesh: ka: 16 (over y_hi, x, core), fft: 16 (over y_lo, z).
Axes of the slice: x: 4, y: 4 (y_hi: 2, y_lo: 2; y = y_hi * 2 + y_lo), z: 8, core: 2. Of those that a mesh axis runs over, the one named last changes fastest.
Arguments:
- psi_val: bfloat16 [16, 2, 4, 442368], P('ka', None, None, 'fft'), may hold values from -6 to 6
- psi_cond: bfloat16 [16, 48, 9216, 128], P('ka', 'fft'), may hold values from -6 to 6
- e_val: float32 [16, 2], replicated, may hold values from -6 to -1
- e_cond: float32 [16, 32], replicated, may hold values from 1 to 8
- occ_val: int32 [16, 2], replicated, may hold values from 1 to 2
- occ_cond: int32 [16, 32], replicated, may hold values from 0 to 1
- umklapp: int32 [16], replicated, may hold values from -2 to 2
- sphere: int32 [4096], replicated, may hold values from 0 to 13823, as said below
Outputs:
- chi0: float32 [4096, 2, 4096], P('ka', None, 'fft')
The draws below stay inside these ranges and needn't reach their ends.
Inputs may be any that keep to these rules, and one draw needn't show every extreme that they name: `sphere`: 4096 distinct indices of the box of 13824 frequencies.
All inputs are finite; a program needn't handle non-finite values.
Results may differ from the reference program's by a relative error of at most 0.02.
Values may be sent and summed in bfloat16 or wider, within the bound.
No kernel may reach another device: no remote copies, remote signals or barrier semaphores. Data moves between devices by JAX's collectives and lax.ppermute only.
A program may use at most 128 MiB of HBM per device.

```python
import math
import jax
import jax.numpy as jnp
from jax import lax

GRID = 96
BOX = 24
NG = 4096
NV = 2
NC = 32
NK = 16
N_KA = 16


def draw_sphere(key, part):
    key = jax.random.fold_in(key, 7)
    first_key, second_key = jax.random.split(key)
    inner_ids = jax.random.permutation(first_key, BOX ** 3 - 2)[:NG - 2].astype(jnp.int32) + 1
    ends = jnp.array([0, BOX ** 3 - 1], jnp.int32)
    picked = jnp.concatenate([ends, inner_ids])
    return jax.random.permutation(second_key, picked).astype(jnp.int32)


def with_ends(result, rng, low, top_value):
    extent = result.shape
    spot = [jax.random.randint(jax.random.fold_in(rng, axis), (), 0, extent[axis]) for axis in range(len(extent))]
    result = result.at[tuple(spot)].set(low)
    longest = extent.index(max(extent))
    spot[longest] = (spot[longest] + 1) % extent[longest]
    return result.at[tuple(spot)].set(top_value)


def shard_levels(stream_key, extent, pieces, least, top_value):
    def one(position, parts):
        draws = jax.random.uniform(jax.random.fold_in(jax.random.fold_in(stream_key, 6), position), (parts,), jnp.float32, least / len(pieces), top_value / len(pieces))
        return jnp.repeat(jnp.exp(draws), extent[position] // parts).reshape((-1,) + (1,) * (len(extent) - position - 1))

    factor_of = one(*pieces[0])
    for cut in pieces[1:]:
        factor_of = factor_of * one(*cut)
    return factor_of


def gaussian(key, extent, deviation, reach, cuts=(), kind=jnp.bfloat16):
    drawn = jax.random.normal(key, extent, jnp.float32) * deviation
    if len(cuts) > 0:
        drawn = shard_levels(key, extent, cuts, -0.22, 0.18) * drawn
    return jnp.clip(drawn, min=-reach, max=reach).astype(kind)


def setup_inputs(seed: int = 0) -> dict:
    streams_of = jax.random.split(jax.random.key(seed), 9)
    psi_val = gaussian(streams_of[0], (NK, NV, 4, GRID // 2 * GRID * GRID), 0.7071, 6.0, ((0, 16), (3, 16)))
    psi_cond = gaussian(streams_of[1], (NK, GRID // 2, GRID * GRID, 4 * NC), 0.7071, 6.0, ((0, 16), (1, 16)))
    e_val = jnp.clip(jax.random.uniform(streams_of[2], (NK, NV), jnp.float32, -6.0, -1.0), -6.0, -1.0)
    e_cond = jnp.clip(jax.random.uniform(streams_of[3], (NK, NC), jnp.float32, 1.0, 8.0), 1.0, 8.0)
    occ_val = with_ends(jax.random.randint(streams_of[4], (NK, NV), 1, 3), jax.random.fold_in(streams_of[4], 1), 1, 2).astype(jnp.int32)
    occ_cond = with_ends(jax.random.randint(streams_of[5], (NK, NC), 0, 2), jax.random.fold_in(streams_of[5], 1), 0, 1).astype(jnp.int32)
    umklapp = with_ends(jax.random.randint(streams_of[6], (NK,), -2, 3), jax.random.fold_in(streams_of[6], 1), -2, 2).astype(jnp.int32)
    sphere = draw_sphere(jax.random.fold_in(streams_of[8], 71), 0)
    return dict(psi_val=psi_val, psi_cond=psi_cond, e_val=e_val, e_cond=e_cond, occ_val=occ_val, occ_cond=occ_cond, umklapp=umklapp, sphere=sphere)


def phase_tables(offset):
    kx_freq = jnp.arange(BOX, dtype=jnp.int32) - BOX // 2 - offset
    x_place = jnp.arange(GRID, dtype=jnp.int32)
    phase_turns = jnp.mod(kx_freq[:, None] * x_place[None, :], GRID).astype(jnp.float32)
    phase_angle = phase_turns * (2.0 * math.pi / GRID)
    return (jnp.cos(phase_angle).astype(jnp.bfloat16), jnp.sin(phase_angle).astype(jnp.bfloat16))

def contract(einsum_form, field_in, table):
    return jnp.einsum(einsum_form, field_in.astype(jnp.float32), table.astype(jnp.float32), precision=lax.Precision.HIGHEST)

def complex_pass(einsum_form, real_part, imag_part, cosine, sine_table):
    out_real = contract(einsum_form, real_part, cosine) + contract(einsum_form, imag_part, sine_table)
    out_imag = contract(einsum_form, imag_part, cosine) - contract(einsum_form, real_part, sine_table)
    return (out_real, out_imag)

def pair_densities(val_bands, cond_bands, offset, sphere):
    cond_grid = cond_bands.reshape(GRID // 2, GRID, GRID, 2, 2, NC)
    cond_grid = jnp.moveaxis(cond_grid, 3, 1).reshape(GRID, GRID, GRID, 2, NC)
    cond_real = cond_grid[..., 0, :].astype(jnp.float32)
    cond_imag = cond_grid[..., 1, :].astype(jnp.float32)
    val_grid = val_bands.reshape(NV, 2, 2, GRID // 2, GRID, GRID)
    val_grid = jnp.transpose(val_grid, (0, 2, 3, 1, 4, 5)).reshape(NV, 2, GRID, GRID, GRID)
    plain_cos, plain_sin = phase_tables(jnp.int32(0))
    shift_cos, shift_sin = phase_tables(offset)
    norm_scale = 1.0 / (GRID * math.sqrt(GRID))

    def one_band(val_band):
        val_real = val_band[0].astype(jnp.float32)[..., None]
        val_imag = val_band[1].astype(jnp.float32)[..., None]
        pair_real = (val_real * cond_real + val_imag * cond_imag).astype(jnp.bfloat16)
        pair_imag = (val_real * cond_imag - val_imag * cond_real).astype(jnp.bfloat16)
        z_real, z_imag = complex_pass('xyzc,fz->xyfc', pair_real, pair_imag, plain_cos, plain_sin)
        y_real, y_imag = complex_pass('xyfc,gy->xgfc', z_real.astype(jnp.bfloat16), z_imag.astype(jnp.bfloat16), plain_cos, plain_sin)
        box_real, box_imag = complex_pass('xgfc,hx->hgfc', y_real.astype(jnp.bfloat16), y_imag.astype(jnp.bfloat16), shift_cos, shift_sin)
        picked_real = box_real.reshape(BOX ** 3, NC)[sphere] * norm_scale
        picked_imag = box_imag.reshape(BOX ** 3, NC)[sphere] * norm_scale
        return jnp.concatenate([picked_real, picked_imag], axis=1).astype(jnp.bfloat16)
    return lax.map(one_band, val_grid)

def reference(psi_val, psi_cond, e_val, e_cond, occ_val, occ_cond, umklapp, sphere):
    step_q = N_KA // 4
    k_points = jnp.arange(NK, dtype=jnp.int32)
    partner = jnp.mod(k_points + step_q, NK)

    def one_point(k_point):
        k_cond = jnp.mod(k_point + step_q, NK)
        return pair_densities(psi_val[k_point], psi_cond[k_cond], umklapp[k_point], sphere)
    rho_all = lax.map(one_point, k_points)
    weight = (occ_val[:, :, None] - occ_cond[partner][:, None, :]).astype(jnp.float32) / ((e_val[:, :, None] - e_cond[partner][:, None, :]) * (NK * NV))
    split_rho = rho_all.reshape(NK, NV, NG, 2, NC).astype(jnp.float32)
    weighted = (split_rho * weight[:, :, None, None, :]).astype(jnp.bfloat16).astype(jnp.float32)
    turned = jnp.stack([-split_rho[:, :, :, 1], split_rho[:, :, :, 0]], axis=3)
    left_side = jnp.transpose(weighted, (2, 0, 1, 3, 4)).reshape(NG, NK * NV * 2 * NC)
    right_side = jnp.transpose(split_rho, (2, 0, 1, 3, 4)).reshape(NG, NK * NV * 2 * NC)
    right_turned = jnp.transpose(turned, (2, 0, 1, 3, 4)).reshape(NG, NK * NV * 2 * NC)
    chi_real = jnp.dot(left_side, right_side.T, preferred_element_type=jnp.float32, precision=lax.Precision.HIGHEST)
    chi_imag = jnp.dot(left_side, right_turned.T, preferred_element_type=jnp.float32, precision=lax.Precision.HIGHEST)
    return jnp.stack([chi_real, chi_imag], axis=1)
```

```python
import math

import jax
import jax.numpy as jnp
import ml_dtypes
import numpy as np
from jax import lax
from jax.experimental import pallas as pl
from jax.experimental.pallas import tpu as pltpu
from jax.sharding import PartitionSpec as P

GRID = 96
BOX = 24
NG = 4096
NV = 2
NC = 32
COLS = 768
ROWS = 256
YCHUNK = 4
PICK = 512


def dft_tables():
    turns = np.mod((np.arange(BOX) - BOX // 2)[:, None] * np.arange(GRID)[None, :], GRID)
    angle = turns.astype(np.float32) * np.float32(2.0 * math.pi / GRID)
    return np.cos(angle), np.sin(angle)


def z_table():
    cosine, sine = dft_tables()
    out = np.zeros((BOX, 2, 2, GRID), np.float32)
    out[:, 0, 0], out[:, 0, 1] = cosine, sine
    out[:, 1, 0], out[:, 1, 1] = -sine, cosine
    return out.reshape(2 * BOX, 2 * GRID).astype(ml_dtypes.bfloat16)


def y_table():
    cosine, sine = dft_tables()
    out = np.zeros((2, 32, 2, GRID), np.float32)
    out[0, :BOX, 0], out[0, :BOX, 1] = cosine, sine
    out[1, :BOX, 0], out[1, :BOX, 1] = -sine, cosine
    return out.reshape(64, 2 * GRID).astype(ml_dtypes.bfloat16)


def val_spread():
    out = np.zeros((NV, 2, 2, 2, 2, NV, NC), np.float32)
    for v in range(NV):
        for p in range(2):
            for i in range(2):
                out[v, p, i, i, p, v, :] = 1.0
    return out.reshape(8, 256).astype(ml_dtypes.bfloat16)


def cond_spread():
    out = np.zeros((2, 2, NC, 2, 2, NV, NC), np.float32)
    for p in range(2):
        for i in range(2):
            for c in range(NC):
                out[p, i, c, i, p, :, c] = 1.0
    return out.reshape(128, 256).astype(ml_dtypes.bfloat16)


def dot(left, right):
    return jnp.dot(left, right, preferred_element_type=jnp.float32)


def field_kernel(val_ref, cond_ref, vs_ref, cs_ref, tz_ref, ty_ref, out_ref, zs_ref):
    points = YCHUNK * GRID

    def z_step(step, carry):
        at = pl.multiple_of(step * points, points)
        val = jnp.concatenate(
            [val_ref[v, :, pl.ds(at, points)].astype(jnp.float32) for v in range(NV)], axis=0
        ).astype(jnp.bfloat16)
        spread = lax.dot_general(
            val, vs_ref[...], (((0,), (0,)), ((), ())), preferred_element_type=jnp.float32
        )
        cond = dot(cond_ref[0, 0, pl.ds(at, points), :], cs_ref[...])
        val_re, val_im = spread[:, :128], spread[:, 128:]
        cond_re, cond_im = cond[:, :128], cond[:, 128:]
        pair_re = (val_re * cond_re + val_im * cond_im).astype(jnp.bfloat16)
        pair_im = (val_re * cond_im - val_im * cond_re).astype(jnp.bfloat16)
        for y in range(0, YCHUNK, 2):
            rhs = jnp.concatenate(
                [
                    jnp.concatenate(
                        [pair_re[(y + u) * GRID : (y + u + 1) * GRID] for u in range(2)], axis=1
                    ),
                    jnp.concatenate(
                        [pair_im[(y + u) * GRID : (y + u + 1) * GRID] for u in range(2)], axis=1
                    ),
                ],
                axis=0,
            )
            z_out = dot(tz_ref[...], rhs)
            for u in range(2):
                zs_ref[pl.ds(step * YCHUNK + y + u, 2 * BOX, stride=GRID), :] = z_out[
                    :, u * 128 : (u + 1) * 128
                ]
        return carry

    lax.fori_loop(0, GRID // YCHUNK, z_step, 0)
    for fz in range(0, BOX, 2):
        rhs = jnp.concatenate(
            [
                zs_ref[(fz + u) * 2 * GRID : (fz + u + 1) * 2 * GRID, :].astype(jnp.bfloat16)
                for u in range(2)
            ],
            axis=1,
        )
        y_out = dot(ty_ref[...], rhs).astype(jnp.bfloat16)
        for u in range(2):
            for i in range(2):
                out_ref[0, (fz + u) * 32 : (fz + u + 1) * 32, i * 128 : (i + 1) * 128] = y_out[
                    i * 32 : (i + 1) * 32, u * 128 : (u + 1) * 128
                ]


def fields(val, cond):
    planes = cond.shape[1]
    return pl.pallas_call(
        field_kernel,
        grid=(planes,),
        in_specs=[
            pl.BlockSpec((NV, 4, GRID * GRID), lambda a: (0, 0, a)),
            pl.BlockSpec((1, 1, GRID * GRID, 128), lambda a: (0, a, 0, 0)),
            pl.BlockSpec((8, 256), lambda a: (0, 0)),
            pl.BlockSpec((128, 256), lambda a: (0, 0)),
            pl.BlockSpec((2 * BOX, 2 * GRID), lambda a: (0, 0)),
            pl.BlockSpec((64, 2 * GRID), lambda a: (0, 0)),
        ],
        out_specs=pl.BlockSpec((1, COLS, 256), lambda a: (a, 0, 0)),
        out_shape=jax.ShapeDtypeStruct((planes, COLS, 256), jnp.bfloat16),
        scratch_shapes=[pltpu.VMEM((2 * BOX * GRID, 128), jnp.float32)],
        compiler_params=pltpu.CompilerParams(vmem_limit_bytes=40 * 2**20),
        cost_estimate=pl.CostEstimate(
            flops=4_000_000_000, bytes_accessed=9_000_000, transcendentals=0
        ),
    )(val, cond, val_spread(), cond_spread(), z_table(), y_table())


def pick_kernel(col_ref, fx_ref, y_ref, xt_ref, out_ref):
    lane = lax.broadcasted_iota(jnp.int32, (PICK, 128), 1)
    column = col_ref[...]
    chosen = jnp.concatenate(
        [
            jnp.where(column == lane + 128 * t, 1.0, 0.0).astype(jnp.bfloat16)
            for t in range(COLS // 128)
        ],
        axis=1,
    )
    freq = jnp.where(fx_ref[...] == lane, 1.0, 0.0).astype(jnp.bfloat16)
    real = jnp.zeros((PICK, 128), jnp.float32)
    imag = jnp.zeros((PICK, 128), jnp.float32)
    for a in range(y_ref.shape[0]):
        got = dot(chosen, y_ref[a])
        phase = dot(freq, xt_ref[:, a * 256 : (a + 1) * 256])
        cosine, sine = phase[:, :128], phase[:, 128:]
        got_re, got_im = got[:, :128], got[:, 128:]
        real = real + cosine * got_re + sine * got_im
        imag = imag + cosine * got_im - sine * got_re
    real = real + pltpu.roll(real, 64, 1)
    imag = imag + pltpu.roll(imag, 64, 1)
    scale = 1.0 / (GRID * math.sqrt(GRID))
    out_ref[...] = (jnp.where(lane < 64, real, imag) * scale).astype(jnp.bfloat16)


def pick(column, freq, field, x_table):
    planes = field.shape[0]
    return pl.pallas_call(
        pick_kernel,
        grid=(NG // PICK,),
        in_specs=[
            pl.BlockSpec((PICK, 128), lambda g: (g, 0)),
            pl.BlockSpec((PICK, 128), lambda g: (g, 0)),
            pl.BlockSpec((planes, COLS, 256), lambda g: (0, 0, 0)),
            pl.BlockSpec((128, planes * 256), lambda g: (0, 0)),
        ],
        out_specs=pl.BlockSpec((PICK, 128), lambda g: (g, 0)),
        out_shape=jax.ShapeDtypeStruct((NG, 128), jnp.bfloat16),
        compiler_params=pltpu.CompilerParams(vmem_limit_bytes=40 * 2**20),
        cost_estimate=pl.CostEstimate(
            flops=8_000_000_000, bytes_accessed=6_000_000, transcendentals=0
        ),
    )(column, freq, field, x_table)


def chi_kernel(row_a_ref, row_b_ref, *refs):
    a_refs, b_refs = refs[:10], refs[10:12]
    weight_ref, out_ref, wa_ref = refs[12:]
    lane = lax.broadcasted_iota(jnp.int32, (ROWS, 128), 1)
    sign = jnp.where(lane < 64, 1.0, -1.0)
    place = 0
    for ref in a_refs:
        for part in range(ref.shape[0] // ROWS):
            row = row_a_ref[place]
            piece = ref[part * ROWS : (part + 1) * ROWS, :].astype(jnp.float32)
            weighted = (piece * weight_ref[pl.ds(row, 1), :]).astype(jnp.bfloat16).astype(jnp.float32)
            wa_ref[row, :ROWS, :] = weighted.astype(jnp.bfloat16)
            wa_ref[row, ROWS:, :] = (pltpu.roll(weighted, 64, 1) * sign).astype(jnp.bfloat16)
            place += 1
    total = jnp.zeros((2 * ROWS, ROWS), jnp.float32)
    place = 0
    for ref in b_refs:
        for part in range(0, ref.shape[0] // ROWS, 2):
            left = jnp.concatenate(
                [wa_ref[row_b_ref[place]], wa_ref[row_b_ref[place + 1]]], axis=1
            )
            right = jnp.concatenate(
                [ref[(part + u) * ROWS : (part + u + 1) * ROWS, :] for u in range(2)], axis=1
            )
            total = total + lax.dot_general(
                left, right, (((1,), (1,)), ((), ())), preferred_element_type=jnp.float32
            )
            place += 2
    out_ref[:, 0, :] = total[:ROWS]
    out_ref[:, 1, :] = total[ROWS:]


def contract(row_a, row_b, a_parts, b_parts, weight):
    smem = pl.BlockSpec(memory_space=pltpu.SMEM)
    vmem = pl.BlockSpec(memory_space=pltpu.VMEM)
    return pl.pallas_call(
        chi_kernel,
        in_specs=[smem, smem] + [vmem] * (len(a_parts) + len(b_parts) + 1),
        out_specs=vmem,
        out_shape=jax.ShapeDtypeStruct((ROWS, 2, ROWS), jnp.float32),
        scratch_shapes=[pltpu.VMEM((16, 2 * ROWS, 128), jnp.bfloat16)],
        compiler_params=pltpu.CompilerParams(vmem_limit_bytes=40 * 2**20),
        cost_estimate=pl.CostEstimate(
            flops=600_000_000, bytes_accessed=4_000_000, transcendentals=0
        ),
    )(row_a, row_b, *a_parts, *b_parts, weight)


def ka_route(move):
    route = []
    for i in range(16):
        y, x, c = move(i // 8, (i // 2) % 4, i % 2)
        route.append((i, (y % 2) * 8 + (x % 4) * 2 + c % 2))
    return route


def fft_route(move):
    route = []
    for i in range(16):
        y, z = move(i // 8, i % 8)
        route.append((i, (y % 2) * 8 + z % 8))
    return route


def gather_columns(rho):
    across = lax.ppermute(rho, "ka", ka_route(lambda y, x, c: (y + 1, x, c)))
    block = jnp.concatenate([rho, across])
    ring = [
        lax.ppermute(block, "ka", ka_route(lambda y, x, c, s=s: (y, x + s, c))) for s in (1, 2, 3)
    ]
    block = jnp.concatenate([block] + ring)
    other = lax.ppermute(block, "ka", ka_route(lambda y, x, c: (y, x, c + 1)))
    row = lax.axis_index("ka")
    y, x, c = row // 8, (row // 2) % 4, row % 2
    places = [
        ((y + dy) % 2) * 8 + ((x - s) % 4) * 2 + (c + dc) % 2
        for dc in range(2)
        for s in range(4)
        for dy in range(2)
    ]
    return [block, other], jnp.stack(places).astype(jnp.int32)


def gather_rows(rho):
    own = lax.ppermute(
        rho, ("ka", "fft"), [(i * 16 + j, j * 16 + i) for i in range(16) for j in range(16)]
    )
    across = lax.ppermute(own, "fft", fft_route(lambda y, z: (y + 1, z)))
    block = jnp.concatenate([own, across])
    spot = lax.axis_index("fft")
    y, z = spot // 8, spot % 8
    parts, places = [own, across], [(y, z), (y + 1, z)]
    up = down = block
    for t in range(1, 4):
        up = lax.ppermute(up, "fft", fft_route(lambda y, z: (y, z + 1)))
        down = lax.ppermute(down, "fft", fft_route(lambda y, z: (y, z - 1)))
        parts += [up, down]
        places += [(y, z - t), (y + 1, z - t), (y, z + t), (y + 1, z + t)]
    parts.append(lax.ppermute(up[:ROWS], "fft", fft_route(lambda y, z: (y, z + 1))))
    parts.append(lax.ppermute(down[ROWS:], "fft", fft_route(lambda y, z: (y, z - 1))))
    places += [(y, z + 4), (y + 1, z + 4)]
    return parts, jnp.stack([(a % 2) * 8 + b % 8 for a, b in places]).astype(jnp.int32)


def shards(psi_val, psi_cond, e_val, e_cond, occ_val, occ_cond, umklapp, sphere):
    count_k = 16
    step_q = 4
    row = lax.axis_index("ka")
    x_block = lax.axis_index("fft")
    planes = psi_cond.shape[1]
    val = lax.ppermute(
        psi_val, "ka", [(i, (i + step_q) % count_k) for i in range(count_k)]
    )[0]
    k_here = jnp.mod(row - step_q, count_k)

    offset = lax.dynamic_index_in_dim(umklapp, k_here, keepdims=False)
    x_place = 2 * planes * x_block + jnp.arange(2 * planes, dtype=jnp.int32)
    x_freq = jnp.arange(128, dtype=jnp.int32) - BOX // 2 - offset
    turns = jnp.mod(x_freq[:, None] * x_place[None, :], GRID).astype(jnp.float32)
    angle = turns * (2.0 * math.pi / GRID)
    both = jnp.stack(
        [jnp.cos(angle).reshape(128, planes, 2), jnp.sin(angle).reshape(128, planes, 2)], axis=2
    )
    x_table = jnp.broadcast_to(both[..., None], (128, planes, 2, 2, 64)).reshape(128, planes * 256)
    x_table = x_table.astype(jnp.bfloat16)
    plane = sphere % (BOX * BOX)
    column = (plane % BOX) * 32 + plane // BOX
    column = jnp.broadcast_to(column[:, None], (NG, 128))
    freq = jnp.broadcast_to((sphere // (BOX * BOX))[:, None], (NG, 128))

    weight = (occ_val[:, :, None] - jnp.roll(occ_cond, -step_q, 0)[:, None, :]).astype(
        jnp.float32
    ) / ((e_val[:, :, None] - jnp.roll(e_cond, -step_q, 0)[:, None, :]) * (count_k * NV))
    weight = jnp.roll(weight.reshape(count_k, NV * NC), step_q, 0)
    weight = jnp.concatenate([weight, weight], axis=1)

    field = fields(val, psi_cond)
    share = pick(column, freq, field, x_table)
    spread = lax.all_to_all(share.reshape(16, ROWS, 128), "fft", 0, 0)
    rho = spread.astype(jnp.float32).sum(0).astype(jnp.bfloat16)
    b_parts, row_b = gather_columns(rho)
    a_parts, row_a = gather_rows(rho)
    return contract(row_a, row_b, a_parts, b_parts, weight)


def solution(mesh):
    placed = (P("ka", None, None, "fft"), P("ka", "fft", None, None), P(), P(), P(), P(), P(), P())
    return jax.shard_map(
        shards, mesh=mesh, in_specs=placed, out_specs=P("ka", None, "fft"), check_vma=False
    )
```

```python
import math

import jax
import jax.numpy as jnp
import ml_dtypes
import numpy as np
from jax import lax
from jax.experimental import pallas as pl
from jax.experimental.pallas import tpu as pltpu
from jax.sharding import PartitionSpec as P

GRID = 96
BOX = 24
NG = 4096
NV = 2
NC = 32
COLS = 768
ROWS = 256
HALF = 128
YCHUNK = 32
ZROW = 104
PICK = 512


def dft_tables():
    turns = np.mod((np.arange(BOX) - BOX // 2)[:, None] * np.arange(GRID)[None, :], GRID)
    angle = turns.astype(np.float32) * np.float32(2.0 * math.pi / GRID)
    return np.cos(angle), np.sin(angle)


def z_table():
    cosine, sine = dft_tables()
    out = np.zeros((BOX, 2, 2, GRID), np.float32)
    out[:, 0, 0], out[:, 0, 1] = cosine, sine
    out[:, 1, 0], out[:, 1, 1] = -sine, cosine
    return out.reshape(2 * BOX, 2 * GRID).astype(ml_dtypes.bfloat16)


def y_table():
    cosine, sine = dft_tables()
    out = np.zeros((2, 32, 2, GRID), np.float32)
    out[0, :BOX, 0], out[0, :BOX, 1] = cosine, sine
    out[1, :BOX, 0], out[1, :BOX, 1] = -sine, cosine
    return out.reshape(64, 2 * GRID).astype(ml_dtypes.bfloat16)


def val_spread():
    out = np.zeros((NV, 2, 2, 2, 2, NV, NC), np.float32)
    for v in range(NV):
        for p in range(2):
            for i in range(2):
                out[v, p, i, i, p, v, :] = 1.0
    return out.reshape(8, 256).astype(ml_dtypes.bfloat16)


def cond_spread():
    out = np.zeros((2, 2, NC, 2, 2, NV, NC), np.float32)
    for p in range(2):
        for i in range(2):
            for c in range(NC):
                out[p, i, c, i, p, :, c] = 1.0
    return out.reshape(128, 256).astype(ml_dtypes.bfloat16)


def dot(left, right):
    return jnp.dot(left, right, preferred_element_type=jnp.float32)


def field_kernel(val_ref, cond_ref, vs_ref, cs_ref, tz_ref, ty_ref, out_ref, zs_ref, pair_ref):
    points = YCHUNK * GRID
    steps = GRID // YCHUNK

    def pairs(step, slot):
        at = pl.multiple_of(step * points, points)
        val = jnp.concatenate(
            [val_ref[v, :, pl.ds(at, points)].astype(jnp.float32) for v in range(NV)], axis=0
        ).astype(jnp.bfloat16)
        spread = lax.dot_general(
            val, vs_ref[...], (((0,), (0,)), ((), ())), preferred_element_type=jnp.float32
        )
        cond = dot(cond_ref[0, 0, pl.ds(at, points), :], cs_ref[...])
        val_re, val_im = spread[:, :128], spread[:, 128:]
        cond_re, cond_im = cond[:, :128], cond[:, 128:]
        pair_ref[slot, 0] = (val_re * cond_re + val_im * cond_im).astype(jnp.bfloat16)
        pair_ref[slot, 1] = (val_re * cond_im - val_im * cond_re).astype(jnp.bfloat16)

    def z_pass(step, slot):
        for y in range(0, YCHUNK, 2):
            rhs = jnp.concatenate(
                [
                    jnp.concatenate(
                        [pair_ref[slot, i, (y + u) * GRID : (y + u + 1) * GRID] for u in range(2)],
                        axis=1,
                    )
                    for i in range(2)
                ],
                axis=0,
            )
            z_out = dot(tz_ref[...], rhs)
            for u in range(2):
                zs_ref[pl.ds(step * YCHUNK + y + u, 2 * BOX, stride=ZROW), :] = z_out[
                    :, u * 128 : (u + 1) * 128
                ]

    def body(step, carry):
        z_pass(step - 1, (step - 1) % 2)
        pairs(step, step % 2)
        return carry

    pairs(0, 0)
    lax.fori_loop(1, steps, body, 0)
    z_pass(steps - 1, (steps - 1) % 2)
    for fz in range(0, BOX, 2):
        rhs = jnp.concatenate(
            [
                jnp.concatenate(
                    [
                        zs_ref[pl.ds(((fz + u) * 2 + i) * ZROW, GRID), :].astype(jnp.bfloat16)
                        for i in range(2)
                    ],
                    axis=0,
                )
                for u in range(2)
            ],
            axis=1,
        )
        y_out = dot(ty_ref[...], rhs).astype(jnp.bfloat16)
        for u in range(2):
            for i in range(2):
                out_ref[0, (fz + u) * 32 : (fz + u + 1) * 32, i * 128 : (i + 1) * 128] = y_out[
                    i * 32 : (i + 1) * 32, u * 128 : (u + 1) * 128
                ]


def fields(val, cond):
    planes = cond.shape[1]
    return pl.pallas_call(
        field_kernel,
        grid=(planes,),
        in_specs=[
            pl.BlockSpec((NV, 4, GRID * GRID), lambda a: (0, 0, a)),
            pl.BlockSpec((1, 1, GRID * GRID, 128), lambda a: (0, a, 0, 0)),
            pl.BlockSpec((8, 256), lambda a: (0, 0)),
            pl.BlockSpec((128, 256), lambda a: (0, 0)),
            pl.BlockSpec((2 * BOX, 2 * GRID), lambda a: (0, 0)),
            pl.BlockSpec((64, 2 * GRID), lambda a: (0, 0)),
        ],
        out_specs=pl.BlockSpec((1, COLS, 256), lambda a: (a, 0, 0)),
        out_shape=jax.ShapeDtypeStruct((planes, COLS, 256), jnp.bfloat16),
        scratch_shapes=[
            pltpu.VMEM((2 * BOX * ZROW, 128), jnp.float32),
            pltpu.VMEM((2, 2, YCHUNK * GRID, 128), jnp.bfloat16),
        ],
        compiler_params=pltpu.CompilerParams(vmem_limit_bytes=60 * 2**20),
        cost_estimate=pl.CostEstimate(
            flops=4_000_000_000, bytes_accessed=9_000_000, transcendentals=0
        ),
    )(val, cond, val_spread(), cond_spread(), z_table(), y_table())


def pick_kernel(col_ref, fx_ref, y_ref, xt_ref, out_ref):
    lane = lax.broadcasted_iota(jnp.int32, (PICK, 128), 1)
    column = col_ref[...]
    chosen = jnp.concatenate(
        [
            jnp.where(column == lane + 128 * t, 1.0, 0.0).astype(jnp.bfloat16)
            for t in range(COLS // 128)
        ],
        axis=1,
    )
    freq = jnp.where(fx_ref[...] == lane, 1.0, 0.0).astype(jnp.bfloat16)
    real = jnp.zeros((PICK, 128), jnp.float32)
    imag = jnp.zeros((PICK, 128), jnp.float32)
    for a in range(y_ref.shape[0]):
        got = dot(chosen, y_ref[a])
        phase = dot(freq, xt_ref[:, a * 256 : (a + 1) * 256])
        cosine, sine = phase[:, :128], phase[:, 128:]
        got_re, got_im = got[:, :128], got[:, 128:]
        real = real + cosine * got_re + sine * got_im
        imag = imag + cosine * got_im - sine * got_re
    real = real + pltpu.roll(real, 64, 1)
    imag = imag + pltpu.roll(imag, 64, 1)
    scale = 1.0 / (GRID * math.sqrt(GRID))
    out_ref[...] = (jnp.where(lane < 64, real, imag) * scale).astype(jnp.bfloat16)


def pick(column, freq, field, x_table):
    planes, count = field.shape[0], column.shape[0]
    return pl.pallas_call(
        pick_kernel,
        grid=(count // PICK,),
        in_specs=[
            pl.BlockSpec((PICK, 128), lambda g: (g, 0)),
            pl.BlockSpec((PICK, 128), lambda g: (g, 0)),
            pl.BlockSpec((planes, COLS, 256), lambda g: (0, 0, 0)),
            pl.BlockSpec((128, planes * 256), lambda g: (0, 0)),
        ],
        out_specs=pl.BlockSpec((PICK, 128), lambda g: (g, 0)),
        out_shape=jax.ShapeDtypeStruct((count, 128), jnp.bfloat16),
        compiler_params=pltpu.CompilerParams(vmem_limit_bytes=60 * 2**20),
        cost_estimate=pl.CostEstimate(
            flops=8_000_000_000, bytes_accessed=6_000_000, transcendentals=0
        ),
    )(column, freq, field, x_table)


def chi_kernel(half_ref, row_ref, own_ref, other_ref, near_ref, far_ref, weight_ref, out_ref, wa_ref):
    lane = lax.broadcasted_iota(jnp.int32, (HALF, 128), 1)
    sign = jnp.where(lane < 64, 1.0, -1.0)
    for h, ref in enumerate((own_ref, other_ref)):
        for row in range(ref.shape[0]):
            weighted = ref[row].astype(jnp.float32) * weight_ref[row : row + 1, :]
            weighted = weighted.astype(jnp.bfloat16).astype(jnp.float32)
            wa_ref[row, (2 * h) * HALF : (2 * h + 1) * HALF] = weighted.astype(jnp.bfloat16)
            wa_ref[row, (2 * h + 1) * HALF : (2 * h + 2) * HALF] = (
                pltpu.roll(weighted, 64, 1) * sign
            ).astype(jnp.bfloat16)
    total = jnp.zeros((4 * HALF, ROWS), jnp.float32)
    place = 0
    for ref in (near_ref, far_ref):
        for part in range(0, ref.shape[0] // ROWS, 2):
            left = jnp.concatenate([wa_ref[row_ref[place]], wa_ref[row_ref[place + 1]]], axis=1)
            right = jnp.concatenate(
                [ref[(part + u) * ROWS : (part + u + 1) * ROWS, :] for u in range(2)], axis=1
            )
            total = total + lax.dot_general(
                left, right, (((1,), (1,)), ((), ())), preferred_element_type=jnp.float32
            )
            place += 2
    for h in range(2):
        at = pl.multiple_of((half_ref[0] + h) % 2 * HALF, HALF)
        for i in range(2):
            out_ref[pl.ds(at, HALF), i, :] = total[(2 * h + i) * HALF : (2 * h + i + 1) * HALF]


def contract(half, row, own, other, near, far, weight):
    smem = pl.BlockSpec(memory_space=pltpu.SMEM)
    vmem = pl.BlockSpec(memory_space=pltpu.VMEM)
    return pl.pallas_call(
        chi_kernel,
        in_specs=[smem, smem] + [vmem] * 5,
        out_specs=vmem,
        out_shape=jax.ShapeDtypeStruct((ROWS, 2, ROWS), jnp.float32),
        scratch_shapes=[pltpu.VMEM((16, 4 * HALF, 128), jnp.bfloat16)],
        compiler_params=pltpu.CompilerParams(vmem_limit_bytes=40 * 2**20),
        cost_estimate=pl.CostEstimate(
            flops=600_000_000, bytes_accessed=4_000_000, transcendentals=0
        ),
    )(half, row, own, other, near, far, weight)


def ka_route(move):
    route = []
    for i in range(16):
        y, x, c = move(i // 8, (i // 2) % 4, i % 2)
        route.append((i, (y % 2) * 8 + (x % 4) * 2 + c % 2))
    return route


def fft_route(move):
    route = []
    for i in range(16):
        y, z = move(i // 8, i % 8)
        route.append((i, (y % 2) * 8 + z % 8))
    return route


def gather_columns(rho):
    across = lax.ppermute(rho, "ka", ka_route(lambda y, x, c: (y + 1, x, c)))
    block = jnp.concatenate([rho, across])
    ring = [
        lax.ppermute(block, "ka", ka_route(lambda y, x, c, s=s: (y, x + s, c))) for s in (1, 2, 3)
    ]
    block = jnp.concatenate([block] + ring)
    other = lax.ppermute(block, "ka", ka_route(lambda y, x, c: (y, x, c + 1)))
    row = lax.axis_index("ka")
    y, x, c = row // 8, (row // 2) % 4, row % 2
    places = [
        ((y + dy) % 2) * 8 + ((x - s) % 4) * 2 + (c + dc) % 2
        for dc in range(2)
        for s in range(4)
        for dy in range(2)
    ]
    return [block, other], jnp.stack(places).astype(jnp.int32)


def gather_rows(own):
    halves = own.reshape(2, 1, HALF, 128)
    copies = jnp.broadcast_to(halves, (2, 8, HALF, 128)).reshape(16, HALF, 128)
    mine = lax.all_to_all(copies, "fft", 0, 0)
    other = lax.ppermute(mine, "fft", fft_route(lambda y, z: (y + 1, z)))
    return mine, other


def shards(psi_val, psi_cond, e_val, e_cond, occ_val, occ_cond, umklapp, sphere):
    count_k = 16
    step_q = 4
    row = lax.axis_index("ka")
    x_block = lax.axis_index("fft")
    planes = psi_cond.shape[1]
    val = lax.ppermute(
        psi_val, "ka", [(i, (i + step_q) % count_k) for i in range(count_k)]
    )[0]
    k_here = jnp.mod(row - step_q, count_k)

    offset = lax.dynamic_index_in_dim(umklapp, k_here, keepdims=False)
    x_place = 2 * planes * x_block + jnp.arange(2 * planes, dtype=jnp.int32)
    x_freq = jnp.arange(128, dtype=jnp.int32) - BOX // 2 - offset
    turns = jnp.mod(x_freq[:, None] * x_place[None, :], GRID).astype(jnp.float32)
    angle = turns * (2.0 * math.pi / GRID)
    both = jnp.stack(
        [jnp.cos(angle).reshape(128, planes, 2), jnp.sin(angle).reshape(128, planes, 2)], axis=2
    )
    x_table = jnp.broadcast_to(both[..., None], (128, planes, 2, 2, 64)).reshape(128, planes * 256)
    x_table = x_table.astype(jnp.bfloat16)
    half = x_block // 8
    blocks = sphere.reshape(16, 2, HALF)

    def places(part):
        index = lax.dynamic_index_in_dim(blocks, part, 1, keepdims=False).reshape(NG // 2)
        plane = index % (BOX * BOX)
        column = (plane % BOX) * 32 + plane // BOX
        freq = index // (BOX * BOX)
        return [jnp.broadcast_to(a[:, None], (NG // 2, 128)) for a in (column, freq)]

    away, home = places(1 - half), places(half)

    weight = (occ_val[:, :, None] - jnp.roll(occ_cond, -step_q, 0)[:, None, :]).astype(
        jnp.float32
    ) / ((e_val[:, :, None] - jnp.roll(e_cond, -step_q, 0)[:, None, :]) * (count_k * NV))
    weight = jnp.roll(weight.reshape(count_k, NV * NC), step_q, 0)
    weight = jnp.concatenate([weight, weight], axis=1)

    val, away, home, x_table, weight = lax.optimization_barrier(
        (val, away, home, x_table, weight)
    )
    field = fields(val, psi_cond)
    sent = pick(away[0], away[1], field, x_table)
    came = lax.ppermute(sent, "fft", fft_route(lambda y, z: (y + 1, z)))
    kept = pick(home[0], home[1], field, x_table)
    share = (kept.astype(jnp.float32) + came.astype(jnp.float32)).astype(jnp.bfloat16)
    spread = lax.all_to_all(share.reshape(16, HALF, 128), "fft", 0, 0)
    rho = spread.reshape(2, 8, HALF, 128).astype(jnp.float32).sum(1).astype(jnp.bfloat16)
    rho = rho.reshape(ROWS, 128)
    turned = lax.ppermute(
        rho, ("ka", "fft"), [(i * 16 + j, j * 16 + i) for i in range(16) for j in range(16)]
    )
    (near, far), row_b = gather_columns(rho)
    mine, other = gather_rows(turned)
    return contract(half[None].astype(jnp.int32), row_b, mine, other, near, far, weight)


def solution(mesh):
    placed = (P("ka", None, None, "fft"), P("ka", "fft", None, None), P(), P(), P(), P(), P(), P())
    return jax.shard_map(
        shards, mesh=mesh, in_specs=placed, out_specs=P("ka", None, "fft"), check_vma=False
    )
```

```python
import math

import jax
import jax.numpy as jnp
import ml_dtypes
import numpy as np
from jax import lax
from jax.experimental import pallas as pl
from jax.experimental.pallas import tpu as pltpu
from jax.sharding import PartitionSpec as P

GRID = 96
BOX = 24
NG = 4096
NV = 2
NC = 32
COLS = 768
ROWS = 256
HALF = 128
YCHUNK = 32
ZROW = 104
PICK = 256


def dft_tables():
    turns = np.mod((np.arange(BOX) - BOX // 2)[:, None] * np.arange(GRID)[None, :], GRID)
    angle = turns.astype(np.float32) * np.float32(2.0 * math.pi / GRID)
    return np.cos(angle), np.sin(angle)


def z_table():
    cosine, sine = dft_tables()
    out = np.zeros((BOX, 2, 2, GRID), np.float32)
    out[:, 0, 0], out[:, 0, 1] = cosine, sine
    out[:, 1, 0], out[:, 1, 1] = -sine, cosine
    return out.reshape(2 * BOX, 2 * GRID).astype(ml_dtypes.bfloat16)


def y_table():
    cosine, sine = dft_tables()
    out = np.zeros((2, 32, 2, GRID), np.float32)
    out[0, :BOX, 0], out[0, :BOX, 1] = cosine, sine
    out[1, :BOX, 0], out[1, :BOX, 1] = -sine, cosine
    return out.reshape(64, 2 * GRID).astype(ml_dtypes.bfloat16)


def val_spread():
    out = np.zeros((NV, 2, 2, 2, 2, NV, NC), np.float32)
    for v in range(NV):
        for p in range(2):
            for i in range(2):
                out[v, p, i, i, p, v, :] = 1.0
    return out.reshape(8, 256).astype(ml_dtypes.bfloat16)


def cond_spread():
    out = np.zeros((2, 2, NC, 2, 2, NV, NC), np.float32)
    for p in range(2):
        for i in range(2):
            for c in range(NC):
                out[p, i, c, i, p, :, c] = 1.0
    return out.reshape(128, 256).astype(ml_dtypes.bfloat16)


def dot(left, right):
    return jnp.dot(left, right, preferred_element_type=jnp.float32)


def field_kernel(
    val_ref, cond_ref, vs_ref, cs_ref, tz_ref, ty_ref, out_ref, zs_ref, pair_ref, y_ref
):
    points = YCHUNK * GRID
    steps = GRID // YCHUNK

    def pairs(step, slot):
        at = pl.multiple_of(step * points, points)
        val = jnp.concatenate(
            [val_ref[v, :, pl.ds(at, points)].astype(jnp.float32) for v in range(NV)], axis=0
        ).astype(jnp.bfloat16)
        spread = lax.dot_general(
            val, vs_ref[...], (((0,), (0,)), ((), ())), preferred_element_type=jnp.float32
        )
        cond = dot(cond_ref[0, 0, pl.ds(at, points), :], cs_ref[...])
        val_re, val_im = spread[:, :128], spread[:, 128:]
        cond_re, cond_im = cond[:, :128], cond[:, 128:]
        pair_ref[slot, 0] = (val_re * cond_re + val_im * cond_im).astype(jnp.bfloat16)
        pair_ref[slot, 1] = (val_re * cond_im - val_im * cond_re).astype(jnp.bfloat16)

    def z_pass(step, slot):
        for y in range(0, YCHUNK, 2):
            rhs = jnp.concatenate(
                [
                    jnp.concatenate(
                        [pair_ref[slot, i, (y + u) * GRID : (y + u + 1) * GRID] for u in range(2)],
                        axis=1,
                    )
                    for i in range(2)
                ],
                axis=0,
            )
            z_out = dot(tz_ref[...], rhs)
            for u in range(2):
                zs_ref[pl.ds(step * YCHUNK + y + u, 2 * BOX, stride=ZROW), :] = z_out[
                    :, u * 128 : (u + 1) * 128
                ]

    def body(step, carry):
        z_pass(step - 1, (step - 1) % 2)
        pairs(step, step % 2)
        return carry

    pairs(0, 0)
    lax.fori_loop(1, steps, body, 0)
    z_pass(steps - 1, (steps - 1) % 2)
    for fz in range(0, BOX, 2):
        rhs = jnp.concatenate(
            [
                jnp.concatenate(
                    [
                        zs_ref[pl.ds(((fz + u) * 2 + i) * ZROW, GRID), :].astype(jnp.bfloat16)
                        for i in range(2)
                    ],
                    axis=0,
                )
                for u in range(2)
            ],
            axis=1,
        )
        y_out = dot(ty_ref[...], rhs).astype(jnp.bfloat16)
        for u in range(2):
            for i in range(2):
                y_ref[(fz + u) * 32 : (fz + u + 1) * 32, i * 128 : (i + 1) * 128] = y_out[
                    i * 32 : (i + 1) * 32, u * 128 : (u + 1) * 128
                ]
    out_ref[0] = y_ref[...].T


def fields(val, cond):
    planes = cond.shape[1]
    return pl.pallas_call(
        field_kernel,
        grid=(planes,),
        in_specs=[
            pl.BlockSpec((NV, 4, GRID * GRID), lambda a: (0, 0, a)),
            pl.BlockSpec((1, 1, GRID * GRID, 128), lambda a: (0, a, 0, 0)),
            pl.BlockSpec((8, 256), lambda a: (0, 0)),
            pl.BlockSpec((128, 256), lambda a: (0, 0)),
            pl.BlockSpec((2 * BOX, 2 * GRID), lambda a: (0, 0)),
            pl.BlockSpec((64, 2 * GRID), lambda a: (0, 0)),
        ],
        out_specs=pl.BlockSpec((1, 256, COLS), lambda a: (a, 0, 0)),
        out_shape=jax.ShapeDtypeStruct((planes, 256, COLS), jnp.bfloat16),
        scratch_shapes=[
            pltpu.VMEM((2 * BOX * ZROW, 128), jnp.float32),
            pltpu.VMEM((2, 2, YCHUNK * GRID, 128), jnp.bfloat16),
            pltpu.VMEM((COLS, 256), jnp.bfloat16),
        ],
        compiler_params=pltpu.CompilerParams(vmem_limit_bytes=60 * 2**20),
        cost_estimate=pl.CostEstimate(
            flops=4_000_000_000, bytes_accessed=9_000_000, transcendentals=0
        ),
    )(val, cond, val_spread(), cond_spread(), z_table(), y_table())


def pick_kernel(col_ref, fx_ref, y_ref, xt_ref, out_ref):
    planes = y_ref.shape[0] // 256

    def tile(step, carry):
        at = pl.multiple_of(step * PICK, PICK)
        spot = lax.broadcasted_iota(jnp.int32, (COLS, PICK), 0)
        chosen = jnp.where(col_ref[:, pl.ds(at, PICK)] == spot, 1.0, 0.0).astype(jnp.bfloat16)
        freq = jnp.where(fx_ref[:, pl.ds(at, PICK)] == spot[:32], 1.0, 0.0).astype(jnp.bfloat16)
        phase = dot(xt_ref[...], freq)
        got = dot(y_ref[...], chosen)
        real = jnp.zeros((64, PICK), jnp.float32)
        imag = jnp.zeros((64, PICK), jnp.float32)
        for a in range(planes):
            for p in range(2):
                cosine = phase[a * 2 + p : a * 2 + p + 1]
                sine = phase[8 + a * 2 + p : 9 + a * 2 + p]
                got_re = got[a * 256 + p * 64 : a * 256 + (p + 1) * 64]
                got_im = got[a * 256 + 128 + p * 64 : a * 256 + 128 + (p + 1) * 64]
                real = real + cosine * got_re + sine * got_im
                imag = imag + cosine * got_im - sine * got_re
        scale = 1.0 / (GRID * math.sqrt(GRID))
        both = (jnp.concatenate([real, imag], axis=0) * scale).astype(jnp.bfloat16)
        out_ref[pl.ds(at, PICK), :] = both.T
        return carry

    lax.fori_loop(0, out_ref.shape[0] // PICK, tile, 0)


def pick(column, freq, field, x_table):
    count = column.shape[1]
    vmem = pl.BlockSpec(memory_space=pltpu.VMEM)
    return pl.pallas_call(
        pick_kernel,
        in_specs=[vmem] * 4,
        out_specs=vmem,
        out_shape=jax.ShapeDtypeStruct((count, 128), jnp.bfloat16),
        compiler_params=pltpu.CompilerParams(vmem_limit_bytes=40 * 2**20),
        cost_estimate=pl.CostEstimate(
            flops=3_000_000_000, bytes_accessed=2_000_000, transcendentals=0
        ),
    )(column, freq, field, x_table)


def chi_kernel(half_ref, row_a_ref, row_ref, own_ref, other_ref, near_ref, far_ref, weight_ref, out_ref, wa_ref):
    lane = lax.broadcasted_iota(jnp.int32, (HALF, 128), 1)
    sign = jnp.where(lane < 64, 1.0, -1.0)
    for h, ref in enumerate((own_ref, other_ref)):
        for row in range(ref.shape[0]):
            k_row = row_a_ref[row]
            weighted = ref[row].astype(jnp.float32) * weight_ref[pl.ds(k_row, 1), :]
            weighted = weighted.astype(jnp.bfloat16).astype(jnp.float32)
            wa_ref[k_row, (2 * h) * HALF : (2 * h + 1) * HALF] = weighted.astype(jnp.bfloat16)
            wa_ref[k_row, (2 * h + 1) * HALF : (2 * h + 2) * HALF] = (
                pltpu.roll(weighted, 64, 1) * sign
            ).astype(jnp.bfloat16)
    total = jnp.zeros((4 * HALF, ROWS), jnp.float32)
    place = 0
    for ref in (near_ref, far_ref):
        for part in range(0, ref.shape[0] // ROWS, 2):
            left = jnp.concatenate([wa_ref[row_ref[place]], wa_ref[row_ref[place + 1]]], axis=1)
            right = jnp.concatenate(
                [ref[(part + u) * ROWS : (part + u + 1) * ROWS, :] for u in range(2)], axis=1
            )
            total = total + lax.dot_general(
                left, right, (((1,), (1,)), ((), ())), preferred_element_type=jnp.float32
            )
            place += 2
    for h in range(2):
        at = pl.multiple_of((half_ref[0] + h) % 2 * HALF, HALF)
        for i in range(2):
            out_ref[pl.ds(at, HALF), i, :] = total[(2 * h + i) * HALF : (2 * h + i + 1) * HALF]


def contract(half, row_a, row, own, other, near, far, weight):
    smem = pl.BlockSpec(memory_space=pltpu.SMEM)
    vmem = pl.BlockSpec(memory_space=pltpu.VMEM)
    return pl.pallas_call(
        chi_kernel,
        in_specs=[smem] * 3 + [vmem] * 5,
        out_specs=vmem,
        out_shape=jax.ShapeDtypeStruct((ROWS, 2, ROWS), jnp.float32),
        scratch_shapes=[pltpu.VMEM((16, 4 * HALF, 128), jnp.bfloat16)],
        compiler_params=pltpu.CompilerParams(vmem_limit_bytes=40 * 2**20),
        cost_estimate=pl.CostEstimate(
            flops=600_000_000, bytes_accessed=4_000_000, transcendentals=0
        ),
    )(half, row_a, row, own, other, near, far, weight)


def ka_route(move):
    route = []
    for i in range(16):
        y, x, c = move(i // 8, (i // 2) % 4, i % 2)
        route.append((i, (y % 2) * 8 + (x % 4) * 2 + c % 2))
    return route


def fft_route(move):
    route = []
    for i in range(16):
        y, z = move(i // 8, i % 8)
        route.append((i, (y % 2) * 8 + z % 8))
    return route


def mesh_route(move):
    route = []
    for k in range(16):
        for f in range(16):
            to_k, to_f = move(k, f)
            route.append((k * 16 + f, to_k * 16 + to_f))
    return route


def column_places():
    row = lax.axis_index("ka")
    y, x, c = row // 8, (row // 2) % 4, row % 2
    places = [
        ((y + dy) % 2) * 8 + ((x - s) % 4) * 2 + (c + dc) % 2
        for dc in range(2)
        for s in range(4)
        for dy in range(2)
    ]
    return jnp.stack(places).astype(jnp.int32)


def shards(psi_val, psi_cond, e_val, e_cond, occ_val, occ_cond, umklapp, sphere):
    count_k = 16
    step_q = 4
    row = lax.axis_index("ka")
    x_block = lax.axis_index("fft")
    planes = psi_cond.shape[1]
    val = lax.ppermute(
        psi_val, "ka", [(i, (i + step_q) % count_k) for i in range(count_k)]
    )[0]
    k_here = jnp.mod(row - step_q, count_k)

    offset = lax.dynamic_index_in_dim(umklapp, k_here, keepdims=False)
    x_place = 2 * planes * x_block + jnp.arange(8, dtype=jnp.int32)
    x_freq = jnp.arange(32, dtype=jnp.int32) - BOX // 2 - offset
    turns = jnp.mod(x_place[:, None] * x_freq[None, :], GRID).astype(jnp.float32)
    angle = turns * (2.0 * math.pi / GRID)
    x_table = jnp.concatenate([jnp.cos(angle), jnp.sin(angle)]).astype(jnp.bfloat16)
    half = x_block // 8
    others = jnp.arange(16, dtype=jnp.int32) ^ row
    blocks = jnp.take(sphere.reshape(16, 2, HALF), others, axis=0)

    def places(part):
        index = lax.dynamic_index_in_dim(blocks, part, 1, keepdims=False).reshape(1, NG // 2)
        plane = index % (BOX * BOX)
        return (plane % BOX) * 32 + plane // BOX, index // (BOX * BOX)

    away, home = places(1 - half), places(half)
    val_occ = jnp.roll(occ_val, step_q, 0)[:, :, None]
    val_energy = jnp.roll(e_val, step_q, 0)[:, :, None]
    weight = (val_occ - occ_cond[:, None, :]).astype(jnp.float32) / (
        (val_energy - e_cond[:, None, :]) * (count_k * NV)
    )
    weight = weight.reshape(count_k, NV * NC)
    weight = jnp.concatenate([weight, weight], axis=1)
    row_b = column_places()

    val, away, home, x_table, weight, others, row_b = lax.optimization_barrier(
        (val, away, home, x_table, weight, others, row_b)
    )
    field = fields(val, psi_cond).reshape(planes * 256, COLS)
    sent = pick(away[0], away[1], field, x_table)
    came = lax.ppermute(sent, "fft", fft_route(lambda y, z: (y + 1, z)))
    kept = pick(home[0], home[1], field, x_table)
    share = (kept.astype(jnp.float32) + came.astype(jnp.float32)).astype(jnp.bfloat16)
    spread = lax.all_to_all(share.reshape(16, HALF, 128), "fft", 0, 0)
    rho = spread.reshape(2, 8, HALF, 128).astype(jnp.float32).sum(1).astype(jnp.bfloat16)
    rho = rho.reshape(ROWS, 128)
    by_row = lax.ppermute(rho, ("ka", "fft"), mesh_route(lambda k, f: (k ^ f, f)))
    by_column = lax.ppermute(rho, ("ka", "fft"), mesh_route(lambda k, f: (k, f ^ k)))
    copies = jnp.broadcast_to(by_row.reshape(2, 1, HALF, 128), (2, 8, HALF, 128))
    mine = lax.all_to_all(copies.reshape(16, HALF, 128), "fft", 0, 0)
    across = lax.ppermute(by_column, "ka", ka_route(lambda y, x, c: (y + 1, x, c)))
    block = jnp.concatenate([by_column, across])
    ring = [
        lax.ppermute(block, "ka", ka_route(lambda y, x, c, s=s: (y, x + s, c))) for s in (1, 2, 3)
    ]
    near = jnp.concatenate([block] + ring)
    near, mine = lax.optimization_barrier((near, mine))
    other = lax.ppermute(mine, "fft", fft_route(lambda y, z: (y + 1, z)))
    far = lax.ppermute(near, "ka", ka_route(lambda y, x, c: (y, x, c + 1)))
    return contract(
        half[None].astype(jnp.int32), others, row_b, mine, other, near, far, weight
    )


def solution(mesh):
    placed = (P("ka", None, None, "fft"), P("ka", "fft", None, None), P(), P(), P(), P(), P(), P())
    return jax.shard_map(
        shards, mesh=mesh, in_specs=placed, out_specs=P("ka", None, "fft"), check_vma=False
    )
```

```python
import functools
import math

import jax
import jax.numpy as jnp
import ml_dtypes
import numpy as np
from jax import lax
from jax.experimental import pallas as pl
from jax.experimental.pallas import tpu as pltpu
from jax.sharding import PartitionSpec as P

GRID = 96
BOX = 24
NG = 4096
NV = 2
NC = 32
COLS = 768
ROWS = 256
HALF = 128
YCHUNK = 32
ZROW = 104
PICK = 256


def dft_tables():
    turns = np.mod((np.arange(BOX) - BOX // 2)[:, None] * np.arange(GRID)[None, :], GRID)
    angle = turns.astype(np.float32) * np.float32(2.0 * math.pi / GRID)
    return np.cos(angle), np.sin(angle)


def z_table():
    cosine, sine = dft_tables()
    out = np.zeros((BOX, 2, 2, GRID), np.float32)
    out[:, 0, 0], out[:, 0, 1] = cosine, sine
    out[:, 1, 0], out[:, 1, 1] = -sine, cosine
    return out.reshape(2 * BOX, 2 * GRID).astype(ml_dtypes.bfloat16)


def y_table():
    cosine, sine = dft_tables()
    out = np.zeros((2, 32, 2, GRID), np.float32)
    out[0, :BOX, 0], out[0, :BOX, 1] = cosine, sine
    out[1, :BOX, 0], out[1, :BOX, 1] = -sine, cosine
    return out.reshape(64, 2 * GRID).astype(ml_dtypes.bfloat16)


def val_spread():
    out = np.zeros((NV, 2, 2, 2, 2, NV, NC), np.float32)
    for v in range(NV):
        for p in range(2):
            for i in range(2):
                out[v, p, i, i, p, v, :] = 1.0
    return out.reshape(8, 256).astype(ml_dtypes.bfloat16)


def cond_spread():
    out = np.zeros((2, 2, NC, 2, 2, NV, NC), np.float32)
    for p in range(2):
        for i in range(2):
            for c in range(NC):
                out[p, i, c, i, p, :, c] = 1.0
    return out.reshape(128, 256).astype(ml_dtypes.bfloat16)


def dot(left, right):
    return jnp.dot(left, right, preferred_element_type=jnp.float32)


def tables():
    out = np.zeros((128, 256), ml_dtypes.bfloat16)
    out[:64, : 2 * GRID] = y_table()
    out[64:112, : 2 * GRID] = z_table()
    out[112:120] = val_spread()
    return out


def spread_kernel(cond_ref, cs_ref, out_ref):
    out_ref[0] = dot(cond_ref[0, 0], cs_ref[...]).astype(jnp.bfloat16)


def spread_cond(cond):
    planes, points = cond.shape[1:3]
    chunk = points // 3
    return pl.pallas_call(
        spread_kernel,
        grid=(planes, 3),
        in_specs=[
            pl.BlockSpec((1, 1, chunk, 128), lambda a, g: (0, a, g, 0)),
            pl.BlockSpec((128, 256), lambda a, g: (0, 0)),
        ],
        out_specs=pl.BlockSpec((1, chunk, 256), lambda a, g: (a, g, 0)),
        out_shape=jax.ShapeDtypeStruct((planes, points, 256), jnp.bfloat16),
        compiler_params=pltpu.CompilerParams(vmem_limit_bytes=20 * 2**20),
        cost_estimate=pl.CostEstimate(
            flops=2_000_000_000, bytes_accessed=20_000_000, transcendentals=0
        ),
    )(cond, cond_spread())


def field_kernel(val_ref, cond_ref, table_ref, out_ref, zs_ref, pair_ref, y_ref):
    points = YCHUNK * GRID
    steps = GRID // YCHUNK
    ty = table_ref[:64, : 2 * GRID]
    tz = table_ref[64:112, : 2 * GRID]
    vs = table_ref[112:120, :]

    def pairs(slot):
        val = jnp.concatenate(
            [val_ref[v].astype(jnp.float32) for v in range(NV)], axis=0
        ).astype(jnp.bfloat16)
        spread = lax.dot_general(
            val, vs, (((0,), (0,)), ((), ())), preferred_element_type=jnp.float32
        )
        cond = cond_ref[0].astype(jnp.float32)
        val_re, val_im = spread[:, :128], spread[:, 128:]
        cond_re, cond_im = cond[:, :128], cond[:, 128:]
        pair_ref[slot, 0] = (val_re * cond_re + val_im * cond_im).astype(jnp.bfloat16)
        pair_ref[slot, 1] = (val_re * cond_im - val_im * cond_re).astype(jnp.bfloat16)

    def z_pass(step, slot):
        for y in range(0, YCHUNK, 2):
            rhs = jnp.concatenate(
                [
                    jnp.concatenate(
                        [pair_ref[slot, i, (y + u) * GRID : (y + u + 1) * GRID] for u in range(2)],
                        axis=1,
                    )
                    for i in range(2)
                ],
                axis=0,
            )
            z_out = dot(tz, rhs)
            for u in range(2):
                zs_ref[pl.ds(step * YCHUNK + y + u, 2 * BOX, stride=ZROW), :] = z_out[
                    :, u * 128 : (u + 1) * 128
                ]

    def y_pass():
        for fz in range(0, BOX, 2):
            rhs = jnp.concatenate(
                [
                    jnp.concatenate(
                        [
                            zs_ref[pl.ds(((fz + u) * 2 + i) * ZROW, GRID), :].astype(jnp.bfloat16)
                            for i in range(2)
                        ],
                        axis=0,
                    )
                    for u in range(2)
                ],
                axis=1,
            )
            y_out = dot(ty, rhs).astype(jnp.bfloat16)
            for u in range(2):
                for i in range(2):
                    y_ref[(fz + u) * 32 : (fz + u + 1) * 32, i * 128 : (i + 1) * 128] = y_out[
                        i * 32 : (i + 1) * 32, u * 128 : (u + 1) * 128
                    ]
        out_ref[0] = y_ref[...].T

    step = pl.program_id(1)

    @pl.when(step == 0)
    def _():
        pairs(0)

    @pl.when(step > 0)
    def _():
        z_pass(step - 1, (step - 1) % 2)
        pairs(step % 2)

    @pl.when(step == steps - 1)
    def _():
        z_pass(step, step % 2)
        y_pass()


def fields(val, cond, first):
    planes = val.shape[2] // (GRID * GRID)
    chunks = GRID // YCHUNK
    return pl.pallas_call(
        field_kernel,
        grid=(planes, chunks),
        in_specs=[
            pl.BlockSpec((NV, 4, YCHUNK * GRID), lambda a, g: (0, 0, a * chunks + g)),
            pl.BlockSpec((1, YCHUNK * GRID, 256), lambda a, g: (first + a, g, 0)),
            pl.BlockSpec((128, 256), lambda a, g: (0, 0)),
        ],
        out_specs=pl.BlockSpec((1, 256, COLS), lambda a, g: (a, 0, 0)),
        out_shape=jax.ShapeDtypeStruct((planes, 256, COLS), jnp.bfloat16),
        scratch_shapes=[
            pltpu.VMEM((2 * BOX * ZROW, 128), jnp.float32),
            pltpu.VMEM((2, 2, YCHUNK * GRID, 128), jnp.bfloat16),
            pltpu.VMEM((COLS, 256), jnp.bfloat16),
        ],
        compiler_params=pltpu.CompilerParams(vmem_limit_bytes=24 * 2**20),
        cost_estimate=pl.CostEstimate(
            flops=2_000_000_000, bytes_accessed=3_000_000, transcendentals=0
        ),
    )(val, cond, tables())


def x_phases(planes):
    angle = np.mod(
        np.arange(-BOX // 2 - 2, 32 - BOX // 2 - 2)[None, :] * np.arange(GRID)[:, None], GRID
    ).astype(np.float32) * np.float32(2.0 * math.pi / GRID)
    out = np.zeros((GRID // (2 * planes), 2, 8, 32), np.float32)
    out[:, 0, : 2 * planes] = np.cos(angle).reshape(-1, 2 * planes, 32)
    out[:, 1, : 2 * planes] = np.sin(angle).reshape(-1, 2 * planes, 32)
    return out.reshape(-1, 16, 32).astype(ml_dtypes.bfloat16)


def whole_div(value, by):
    return ((value.astype(jnp.float32) + 0.5) * (1.0 / by)).astype(jnp.int32)


def pick_kernel(first, away, umklapp_ref, sphere_ref, xt_ref, *refs):
    y_refs, out_ref = refs[:-1], refs[-1]
    place = lax.axis_index("fft")
    offset = umklapp_ref[lax.rem(lax.axis_index("ka") + 12, 16)]
    part = lax.rem(place // 8 + (1 if away else 0), 2)
    table = xt_ref[place]

    def tile(step, carry):
        index = jnp.concatenate(
            [
                sphere_ref[pl.ds((first + step * (PICK // HALF) + u) * 2 + part, 1), :]
                for u in range(PICK // HALF)
            ],
            axis=1,
        )
        x_freq = whole_div(index, BOX * BOX)
        plane = index - x_freq * (BOX * BOX)
        y_freq = whole_div(plane, BOX)
        column = (plane - y_freq * BOX) * 32 + y_freq
        spot = lax.broadcasted_iota(jnp.int32, (COLS, PICK), 0)
        chosen = jnp.where(column == spot, 1.0, 0.0).astype(jnp.bfloat16)
        freq = jnp.where(x_freq - offset + 2 == spot[:32], 1.0, 0.0).astype(jnp.bfloat16)
        phase = dot(table, freq)
        real = jnp.zeros((64, PICK), jnp.float32)
        imag = jnp.zeros((64, PICK), jnp.float32)
        a = 0
        for y_ref in y_refs:
            for plane_at in range(y_ref.shape[0]):
                got = dot(y_ref[plane_at], chosen)
                for p in range(2):
                    cosine = phase[a * 2 + p : a * 2 + p + 1]
                    sine = phase[8 + a * 2 + p : 9 + a * 2 + p]
                    got_re = got[p * 64 : (p + 1) * 64]
                    got_im = got[128 + p * 64 : 128 + (p + 1) * 64]
                    real = real + cosine * got_re + sine * got_im
                    imag = imag + cosine * got_im - sine * got_re
                a += 1
        scale = 1.0 / (GRID * math.sqrt(GRID))
        both = (jnp.concatenate([real, imag], axis=0) * scale).astype(jnp.bfloat16)
        out_ref[pl.ds(pl.multiple_of(step * PICK, PICK), PICK), :] = both.T
        return carry

    lax.fori_loop(0, out_ref.shape[0] // PICK, tile, 0)


def pick(first, count, away, umklapp, sphere, planes):
    vmem = pl.BlockSpec(memory_space=pltpu.VMEM)
    return pl.pallas_call(
        functools.partial(pick_kernel, first, away),
        in_specs=[pl.BlockSpec(memory_space=pltpu.SMEM)] + [vmem] * (2 + len(planes)),
        out_specs=vmem,
        out_shape=jax.ShapeDtypeStruct((count * HALF, 128), jnp.bfloat16),
        compiler_params=pltpu.CompilerParams(vmem_limit_bytes=24 * 2**20),
        cost_estimate=pl.CostEstimate(
            flops=100_000_000, bytes_accessed=500_000, transcendentals=0
        ),
    )(umklapp, sphere, x_phases(3), *planes)


def chi_kernel(
    e_val_ref, occ_val_ref, e_cond_ref, occ_cond_ref, own_ref, other_ref, near_ref, far_ref,
    out_ref, wa_ref,
):
    lane = lax.broadcasted_iota(jnp.int32, (1, 128), 1)
    sign = jnp.where(lane < 64, 1.0, -1.0)
    band = (lane // NC) % NV == 0
    e_cond = jnp.concatenate([e_cond_ref[...]] * 4, axis=1)
    occ_cond = jnp.concatenate([occ_cond_ref[...].astype(jnp.float32)] * 4, axis=1)
    for row in range(own_ref.shape[0]):
        k = (row + 12) % 16
        e_val = jnp.where(band, e_val_ref[0, k], e_val_ref[1, k])
        occ_val = jnp.where(band, occ_val_ref[0, k], occ_val_ref[1, k]).astype(jnp.float32)
        weight = (occ_val - occ_cond[row : row + 1]) / (
            (e_val - e_cond[row : row + 1]) * (16 * NV)
        )
        for h, ref in enumerate((own_ref, other_ref)):
            weighted = ref[row].astype(jnp.float32) * weight
            weighted = weighted.astype(jnp.bfloat16).astype(jnp.float32)
            wa_ref[row, (2 * h) * HALF : (2 * h + 1) * HALF] = weighted.astype(jnp.bfloat16)
            wa_ref[row, (2 * h + 1) * HALF : (2 * h + 2) * HALF] = (
                pltpu.roll(weighted, 64, 1) * sign
            ).astype(jnp.bfloat16)
    at = lax.axis_index("ka")
    y, x, c = at // 8, lax.rem(at // 2, 4), lax.rem(at, 2)
    total = jnp.zeros((4 * HALF, ROWS), jnp.float32)
    for dc, ref in enumerate((near_ref, far_ref)):
        for s in range(4):
            rows = [
                lax.rem(y + dy, 2) * 8 + lax.rem(x + 4 - s, 4) * 2 + lax.rem(c + dc, 2)
                for dy in range(2)
            ]
            left = jnp.concatenate([wa_ref[r] for r in rows], axis=1)
            right = jnp.concatenate(
                [ref[(2 * s + u) * ROWS : (2 * s + u + 1) * ROWS, :] for u in range(2)], axis=1
            )
            total = total + lax.dot_general(
                left, right, (((1,), (1,)), ((), ())), preferred_element_type=jnp.float32
            )
    half = lax.axis_index("fft") // 8
    for h in range(2):
        start = pl.multiple_of(lax.rem(half + h, 2) * HALF, HALF)
        for i in range(2):
            out_ref[pl.ds(start, HALF), i, :] = total[(2 * h + i) * HALF : (2 * h + i + 1) * HALF]


def contract(e_val, occ_val, e_cond, occ_cond, own, other, near, far):
    smem = pl.BlockSpec(memory_space=pltpu.SMEM)
    vmem = pl.BlockSpec(memory_space=pltpu.VMEM)
    return pl.pallas_call(
        chi_kernel,
        in_specs=[smem, smem] + [vmem] * 6,
        out_specs=vmem,
        out_shape=jax.ShapeDtypeStruct((ROWS, 2, ROWS), jnp.float32),
        scratch_shapes=[pltpu.VMEM((16, 4 * HALF, 128), jnp.bfloat16)],
        compiler_params=pltpu.CompilerParams(vmem_limit_bytes=24 * 2**20),
        cost_estimate=pl.CostEstimate(
            flops=600_000_000, bytes_accessed=4_000_000, transcendentals=0
        ),
    )(e_val.T, occ_val.T, e_cond, occ_cond, own, other, near, far)


def ka_route(move):
    route = []
    for i in range(16):
        y, x, c = move(i // 8, (i // 2) % 4, i % 2)
        route.append((i, (y % 2) * 8 + (x % 4) * 2 + c % 2))
    return route


def fft_route(move):
    route = []
    for i in range(16):
        y, z = move(i // 8, i % 8)
        route.append((i, (y % 2) * 8 + z % 8))
    return route


def mesh_route(move):
    route = []
    for k in range(16):
        for f in range(16):
            to_k, to_f = move(k, f)
            route.append((k * 16 + f, to_k * 16 + to_f))
    return route


def shards(psi_val, psi_cond, e_val, e_cond, occ_val, occ_cond, umklapp, sphere):
    count_k = 16
    step_q = 4
    planes = psi_cond.shape[1]
    shift = [(i, (i + step_q) % count_k) for i in range(count_k)]
    val = lax.ppermute(psi_val, "ka", shift)[0]
    field = [fields(val, spread_cond(psi_cond), 0)]
    sphere = sphere.reshape(NG // HALF, HALF)
    swap = fft_route(lambda y, z: (y + 1, z))
    came = []
    for at in (0, 8):
        sent = pick(at, 8, True, umklapp, sphere, field)
        sent, *field = lax.optimization_barrier((sent, *field))
        came.append(lax.ppermute(sent, "fft", swap))
    kept = pick(0, 16, False, umklapp, sphere, field)
    came = jnp.concatenate(came)
    share = (kept.astype(jnp.float32) + came.astype(jnp.float32)).astype(jnp.bfloat16)
    spread = lax.all_to_all(share.reshape(16, HALF, 128), "fft", 0, 0)
    rho = spread.reshape(2, 8, HALF, 128).astype(jnp.float32).sum(1).astype(jnp.bfloat16)
    rho = rho.reshape(ROWS, 128)
    own = lax.ppermute(rho, ("ka", "fft"), mesh_route(lambda k, f: (f, k)))
    copies = jnp.broadcast_to(own.reshape(2, 1, HALF, 128), (2, 8, HALF, 128))
    copies, rho = lax.optimization_barrier((copies, rho))
    mine = lax.all_to_all(copies.reshape(16, HALF, 128), "fft", 0, 0)
    across = lax.ppermute(rho, "ka", ka_route(lambda y, x, c: (y + 1, x, c)))
    block = jnp.concatenate([rho, across])
    ring = [
        lax.ppermute(block, "ka", ka_route(lambda y, x, c, s=s: (y, x + s, c))) for s in (1, 2, 3)
    ]
    near = jnp.concatenate([block] + ring)
    near, mine = lax.optimization_barrier((near, mine))
    other = lax.ppermute(mine, "fft", swap)
    far = lax.ppermute(near, "ka", ka_route(lambda y, x, c: (y, x, c + 1)))
    return contract(e_val, occ_val, e_cond, occ_cond, mine, other, near, far)


def solution(mesh):
    placed = (P("ka", None, None, "fft"), P("ka", "fft", None, None), P(), P(), P(), P(), P(), P())
    return jax.shard_map(
        shards, mesh=mesh, in_specs=placed, out_specs=P("ka", None, "fft"), check_vma=False
    )
```

```python
import functools
import math

import jax
import jax.numpy as jnp
import ml_dtypes
import numpy as np
from jax import lax
from jax.experimental import pallas as pl
from jax.experimental.pallas import tpu as pltpu
from jax.sharding import PartitionSpec as P

GRID = 96
BOX = 24
NG = 4096
NV = 2
NC = 32
COLS = 768
ROWS = 256
HALF = 128
YCHUNK = 32
ZROW = 104
PICK = 256


def dft_tables():
    turns = np.mod((np.arange(BOX) - BOX // 2)[:, None] * np.arange(GRID)[None, :], GRID)
    angle = turns.astype(np.float32) * np.float32(2.0 * math.pi / GRID)
    return np.cos(angle), np.sin(angle)


def z_table():
    cosine, sine = dft_tables()
    out = np.zeros((BOX, 2, 2, GRID), np.float32)
    out[:, 0, 0], out[:, 0, 1] = cosine, sine
    out[:, 1, 0], out[:, 1, 1] = -sine, cosine
    return out.reshape(2 * BOX, 2 * GRID).astype(ml_dtypes.bfloat16)


def y_table():
    cosine, sine = dft_tables()
    out = np.zeros((2, 32, 2, GRID), np.float32)
    out[0, :BOX, 0], out[0, :BOX, 1] = cosine, sine
    out[1, :BOX, 0], out[1, :BOX, 1] = -sine, cosine
    return out.reshape(64, 2 * GRID).astype(ml_dtypes.bfloat16)


def val_spread():
    out = np.zeros((NV, 2, 2, 2, 2, NV, NC), np.float32)
    for v in range(NV):
        for p in range(2):
            for i in range(2):
                out[v, p, i, i, p, v, :] = 1.0
    return out.reshape(8, 256).astype(ml_dtypes.bfloat16)


def cond_spread():
    out = np.zeros((2, 2, NC, 2, 2, NV, NC), np.float32)
    for p in range(2):
        for i in range(2):
            for c in range(NC):
                out[p, i, c, i, p, :, c] = 1.0
    return out.reshape(128, 256).astype(ml_dtypes.bfloat16)


def dot(left, right):
    return jnp.dot(left, right, preferred_element_type=jnp.float32)


def tables():
    out = np.zeros((128, 256), ml_dtypes.bfloat16)
    out[:64, : 2 * GRID] = y_table()
    out[64:112, : 2 * GRID] = z_table()
    out[112:120] = val_spread()
    return out


def spread_kernel(cond_ref, cs_ref, out_ref):
    out_ref[0] = dot(cond_ref[0, 0], cs_ref[...]).astype(jnp.bfloat16)


def spread_cond(cond):
    planes, points = cond.shape[1:3]
    chunk = points // 3
    return pl.pallas_call(
        spread_kernel,
        grid=(planes, 3),
        in_specs=[
            pl.BlockSpec((1, 1, chunk, 128), lambda a, g: (0, a, g, 0)),
            pl.BlockSpec((128, 256), lambda a, g: (0, 0)),
        ],
        out_specs=pl.BlockSpec((1, chunk, 256), lambda a, g: (a, g, 0)),
        out_shape=jax.ShapeDtypeStruct((planes, points, 256), jnp.bfloat16),
        compiler_params=pltpu.CompilerParams(vmem_limit_bytes=20 * 2**20),
        cost_estimate=pl.CostEstimate(
            flops=2_000_000_000, bytes_accessed=20_000_000, transcendentals=0
        ),
    )(cond, cond_spread())


def field_kernel(val_ref, cond_ref, table_ref, out_ref, zs_ref, pair_ref, y_ref):
    points = YCHUNK * GRID
    steps = GRID // YCHUNK
    ty = table_ref[:64, : 2 * GRID]
    tz = table_ref[64:112, : 2 * GRID]
    vs = table_ref[112:120, :]

    def pairs(slot):
        val = jnp.concatenate(
            [val_ref[v].astype(jnp.float32) for v in range(NV)], axis=0
        ).astype(jnp.bfloat16)
        spread = lax.dot_general(
            val, vs, (((0,), (0,)), ((), ())), preferred_element_type=jnp.float32
        )
        cond = cond_ref[0].astype(jnp.float32)
        val_re, val_im = spread[:, :128], spread[:, 128:]
        cond_re, cond_im = cond[:, :128], cond[:, 128:]
        pair_ref[slot, 0] = (val_re * cond_re + val_im * cond_im).astype(jnp.bfloat16)
        pair_ref[slot, 1] = (val_re * cond_im - val_im * cond_re).astype(jnp.bfloat16)

    def z_pass(step, slot):
        for y in range(0, YCHUNK, 2):
            rhs = jnp.concatenate(
                [
                    jnp.concatenate(
                        [pair_ref[slot, i, (y + u) * GRID : (y + u + 1) * GRID] for u in range(2)],
                        axis=1,
                    )
                    for i in range(2)
                ],
                axis=0,
            )
            z_out = dot(tz, rhs)
            for u in range(2):
                zs_ref[pl.ds(step * YCHUNK + y + u, 2 * BOX, stride=ZROW), :] = z_out[
                    :, u * 128 : (u + 1) * 128
                ]

    def y_pass():
        for fz in range(0, BOX, 2):
            rhs = jnp.concatenate(
                [
                    jnp.concatenate(
                        [
                            zs_ref[pl.ds(((fz + u) * 2 + i) * ZROW, GRID), :].astype(jnp.bfloat16)
                            for i in range(2)
                        ],
                        axis=0,
                    )
                    for u in range(2)
                ],
                axis=1,
            )
            y_out = dot(ty, rhs).astype(jnp.bfloat16)
            for u in range(2):
                for i in range(2):
                    y_ref[(fz + u) * 32 : (fz + u + 1) * 32, i * 128 : (i + 1) * 128] = y_out[
                        i * 32 : (i + 1) * 32, u * 128 : (u + 1) * 128
                    ]
        out_ref[0] = y_ref[...].T

    step = pl.program_id(1)

    @pl.when(step == 0)
    def _():
        pairs(0)

    @pl.when(step > 0)
    def _():
        z_pass(step - 1, (step - 1) % 2)
        pairs(step % 2)

    @pl.when(step == steps - 1)
    def _():
        z_pass(step, step % 2)
        y_pass()


def fields(val, cond, first):
    planes = val.shape[2] // (GRID * GRID)
    chunks = GRID // YCHUNK
    return pl.pallas_call(
        field_kernel,
        grid=(planes, chunks),
        in_specs=[
            pl.BlockSpec((NV, 4, YCHUNK * GRID), lambda a, g: (0, 0, a * chunks + g)),
            pl.BlockSpec((1, YCHUNK * GRID, 256), lambda a, g: (first + a, g, 0)),
            pl.BlockSpec((128, 256), lambda a, g: (0, 0)),
        ],
        out_specs=pl.BlockSpec((1, 256, COLS), lambda a, g: (a, 0, 0)),
        out_shape=jax.ShapeDtypeStruct((planes, 256, COLS), jnp.bfloat16),
        scratch_shapes=[
            pltpu.VMEM((2 * BOX * ZROW, 128), jnp.float32),
            pltpu.VMEM((2, 2, YCHUNK * GRID, 128), jnp.bfloat16),
            pltpu.VMEM((COLS, 256), jnp.bfloat16),
        ],
        compiler_params=pltpu.CompilerParams(vmem_limit_bytes=24 * 2**20),
        cost_estimate=pl.CostEstimate(
            flops=2_000_000_000, bytes_accessed=3_000_000, transcendentals=0
        ),
    )(val, cond, tables())


def x_phases(planes):
    angle = np.mod(
        np.arange(-BOX // 2 - 2, 32 - BOX // 2 - 2)[None, :] * np.arange(GRID)[:, None], GRID
    ).astype(np.float32) * np.float32(2.0 * math.pi / GRID)
    out = np.zeros((GRID // (2 * planes), 2, 8, 32), np.float32)
    out[:, 0, : 2 * planes] = np.cos(angle).reshape(-1, 2 * planes, 32)
    out[:, 1, : 2 * planes] = np.sin(angle).reshape(-1, 2 * planes, 32)
    return out.reshape(-1, 16, 32).astype(ml_dtypes.bfloat16)


def whole_div(value, by):
    return ((value.astype(jnp.float32) + 0.5) * (1.0 / by)).astype(jnp.int32)


def pick_kernel(first, away, umklapp_ref, sphere_ref, xt_ref, *refs):
    y_refs, out_ref = refs[:-1], refs[-1]
    place = lax.axis_index("fft")
    offset = umklapp_ref[lax.rem(lax.axis_index("ka") + 12, 16)]
    part = lax.rem(place // 8 + (1 if away else 0), 2)
    table = xt_ref[place]

    def tile(step, carry):
        index = jnp.concatenate(
            [
                sphere_ref[pl.ds((first + step * (PICK // HALF) + u) * 2 + part, 1), :]
                for u in range(PICK // HALF)
            ],
            axis=1,
        )
        x_freq = whole_div(index, BOX * BOX)
        plane = index - x_freq * (BOX * BOX)
        y_freq = whole_div(plane, BOX)
        column = (plane - y_freq * BOX) * 32 + y_freq
        spot = lax.broadcasted_iota(jnp.int32, (COLS, PICK), 0)
        chosen = jnp.where(column == spot, 1.0, 0.0).astype(jnp.bfloat16)
        freq = jnp.where(x_freq - offset + 2 == spot[:32], 1.0, 0.0).astype(jnp.bfloat16)
        phase = dot(table, freq)
        real = jnp.zeros((64, PICK), jnp.float32)
        imag = jnp.zeros((64, PICK), jnp.float32)
        a = 0
        for y_ref in y_refs:
            for plane_at in range(y_ref.shape[0]):
                got = dot(y_ref[plane_at], chosen)
                for p in range(2):
                    cosine = phase[a * 2 + p : a * 2 + p + 1]
                    sine = phase[8 + a * 2 + p : 9 + a * 2 + p]
                    got_re = got[p * 64 : (p + 1) * 64]
                    got_im = got[128 + p * 64 : 128 + (p + 1) * 64]
                    real = real + cosine * got_re + sine * got_im
                    imag = imag + cosine * got_im - sine * got_re
                a += 1
        scale = 1.0 / (GRID * math.sqrt(GRID))
        both = (jnp.concatenate([real, imag], axis=0) * scale).astype(jnp.bfloat16)
        out_ref[pl.ds(pl.multiple_of(step * PICK, PICK), PICK), :] = both.T
        return carry

    lax.fori_loop(0, out_ref.shape[0] // PICK, tile, 0, unroll=2)


def pick(first, count, away, umklapp, sphere, planes):
    vmem = pl.BlockSpec(memory_space=pltpu.VMEM)
    return pl.pallas_call(
        functools.partial(pick_kernel, first, away),
        in_specs=[pl.BlockSpec(memory_space=pltpu.SMEM)] + [vmem] * (2 + len(planes)),
        out_specs=vmem,
        out_shape=jax.ShapeDtypeStruct((count * HALF, 128), jnp.bfloat16),
        compiler_params=pltpu.CompilerParams(vmem_limit_bytes=24 * 2**20),
        cost_estimate=pl.CostEstimate(
            flops=100_000_000, bytes_accessed=500_000, transcendentals=0
        ),
    )(umklapp, sphere, x_phases(3), *planes)


def chi_kernel(
    e_val_ref, occ_val_ref, e_cond_ref, occ_cond_ref, own_ref, other_ref, near_ref, far_ref,
    out_ref, wa_ref,
):
    lane = lax.broadcasted_iota(jnp.int32, (1, 128), 1)
    sign = jnp.where(lane < 64, 1.0, -1.0)
    band = (lane // NC) % NV == 0
    e_cond = jnp.concatenate([e_cond_ref[...]] * 4, axis=1)
    occ_cond = jnp.concatenate([occ_cond_ref[...].astype(jnp.float32)] * 4, axis=1)
    for row in range(own_ref.shape[0]):
        k = (row + 12) % 16
        e_val = jnp.where(band, e_val_ref[0, k], e_val_ref[1, k])
        occ_val = jnp.where(band, occ_val_ref[0, k], occ_val_ref[1, k]).astype(jnp.float32)
        weight = (occ_val - occ_cond[row : row + 1]) / (
            (e_val - e_cond[row : row + 1]) * (16 * NV)
        )
        for h, ref in enumerate((own_ref, other_ref)):
            weighted = ref[row].astype(jnp.float32) * weight
            weighted = weighted.astype(jnp.bfloat16).astype(jnp.float32)
            wa_ref[row, (2 * h) * HALF : (2 * h + 1) * HALF] = weighted.astype(jnp.bfloat16)
            wa_ref[row, (2 * h + 1) * HALF : (2 * h + 2) * HALF] = (
                pltpu.roll(weighted, 64, 1) * sign
            ).astype(jnp.bfloat16)
    at = lax.axis_index("ka")
    y, x, c = at // 8, lax.rem(at // 2, 4), lax.rem(at, 2)
    total = jnp.zeros((4 * HALF, ROWS), jnp.float32)
    for dc, ref in enumerate((near_ref, far_ref)):
        for s in range(4):
            rows = [
                lax.rem(y + dy, 2) * 8 + lax.rem(x + 4 - s, 4) * 2 + lax.rem(c + dc, 2)
                for dy in range(2)
            ]
            left = jnp.concatenate([wa_ref[r] for r in rows], axis=1)
            right = jnp.concatenate(
                [ref[(2 * s + u) * ROWS : (2 * s + u + 1) * ROWS, :] for u in range(2)], axis=1
            )
            total = total + lax.dot_general(
                left, right, (((1,), (1,)), ((), ())), preferred_element_type=jnp.float32
            )
    half = lax.axis_index("fft") // 8
    for h in range(2):
        start = pl.multiple_of(lax.rem(half + h, 2) * HALF, HALF)
        for i in range(2):
            out_ref[pl.ds(start, HALF), i, :] = total[(2 * h + i) * HALF : (2 * h + i + 1) * HALF]


def contract(e_val, occ_val, e_cond, occ_cond, own, other, near, far):
    smem = pl.BlockSpec(memory_space=pltpu.SMEM)
    vmem = pl.BlockSpec(memory_space=pltpu.VMEM)
    return pl.pallas_call(
        chi_kernel,
        in_specs=[smem, smem] + [vmem] * 6,
        out_specs=vmem,
        out_shape=jax.ShapeDtypeStruct((ROWS, 2, ROWS), jnp.float32),
        scratch_shapes=[pltpu.VMEM((16, 4 * HALF, 128), jnp.bfloat16)],
        compiler_params=pltpu.CompilerParams(vmem_limit_bytes=24 * 2**20),
        cost_estimate=pl.CostEstimate(
            flops=600_000_000, bytes_accessed=4_000_000, transcendentals=0
        ),
    )(e_val.T, occ_val.T, e_cond, occ_cond, own, other, near, far)


def ka_route(move):
    route = []
    for i in range(16):
        y, x, c = move(i // 8, (i // 2) % 4, i % 2)
        route.append((i, (y % 2) * 8 + (x % 4) * 2 + c % 2))
    return route


def fft_route(move):
    route = []
    for i in range(16):
        y, z = move(i // 8, i % 8)
        route.append((i, (y % 2) * 8 + z % 8))
    return route


def mesh_route(move):
    route = []
    for k in range(16):
        for f in range(16):
            to_k, to_f = move(k, f)
            route.append((k * 16 + f, to_k * 16 + to_f))
    return route


def shards(psi_val, psi_cond, e_val, e_cond, occ_val, occ_cond, umklapp, sphere):
    count_k = 16
    step_q = 4
    planes = psi_cond.shape[1]
    shift = [(i, (i + step_q) % count_k) for i in range(count_k)]
    val = lax.ppermute(psi_val, "ka", shift)[0]
    field = [fields(val, spread_cond(psi_cond), 0)]
    sphere = sphere.reshape(NG // HALF, HALF)
    swap = fft_route(lambda y, z: (y + 1, z))
    shares = []
    sent = [None, None]
    for i, at in enumerate((0, 8)):
        sent[i] = pick(at, 8, True, umklapp, sphere, field)
        sent[i], *field = lax.optimization_barrier((sent[i], *field))
    came = [lax.ppermute(part, "fft", swap) for part in sent]
    for i, at in enumerate((0, 8)):
        kept = pick(at, 8, False, umklapp, sphere, field)
        shares.append((kept.astype(jnp.float32) + came[i].astype(jnp.float32)).astype(jnp.bfloat16))
        shares[i], *field = lax.optimization_barrier((shares[i], *field))
    share = jnp.concatenate(shares)
    spread = lax.all_to_all(share.reshape(16, HALF, 128), "fft", 0, 0)
    rho = spread.reshape(2, 8, HALF, 128).astype(jnp.float32).sum(1).astype(jnp.bfloat16)
    rho = rho.reshape(ROWS, 128)
    own = lax.ppermute(rho, ("ka", "fft"), mesh_route(lambda k, f: (f, k)))
    copies = jnp.broadcast_to(own.reshape(2, 1, HALF, 128), (2, 8, HALF, 128))
    copies, rho = lax.optimization_barrier((copies, rho))
    mine = lax.all_to_all(copies.reshape(16, HALF, 128), "fft", 0, 0)
    across = lax.ppermute(rho, "ka", ka_route(lambda y, x, c: (y + 1, x, c)))
    block = jnp.concatenate([rho, across])
    ring = [
        lax.ppermute(block, "ka", ka_route(lambda y, x, c, s=s: (y, x + s, c))) for s in (1, 2, 3)
    ]
    near = jnp.concatenate([block] + ring)
    near, mine = lax.optimization_barrier((near, mine))
    other = lax.ppermute(mine, "fft", swap)
    far = lax.ppermute(near, "ka", ka_route(lambda y, x, c: (y, x, c + 1)))
    return contract(e_val, occ_val, e_cond, occ_cond, mine, other, near, far)


def solution(mesh):
    placed = (P("ka", None, None, "fft"), P("ka", "fft", None, None), P(), P(), P(), P(), P(), P())
    return jax.shard_map(
        shards, mesh=mesh, in_specs=placed, out_specs=P("ka", None, "fft"), check_vma=False
    )
```

```python
import functools
import math

import jax
import jax.numpy as jnp
import ml_dtypes
import numpy as np
from jax import lax
from jax.experimental import pallas as pl
from jax.experimental.pallas import tpu as pltpu
from jax.sharding import PartitionSpec as P

GRID = 96
BOX = 24
NG = 4096
NV = 2
NC = 32
COLS = 768
ROWS = 256
HALF = 128
YCHUNK = 48
ZROW = 104
PICK = 256


def dft_tables():
    turns = np.mod((np.arange(BOX) - BOX // 2)[:, None] * np.arange(GRID)[None, :], GRID)
    angle = turns.astype(np.float32) * np.float32(2.0 * math.pi / GRID)
    return np.cos(angle), np.sin(angle)


def z_table():
    cosine, sine = dft_tables()
    out = np.zeros((BOX, 2, 2, GRID), np.float32)
    out[:, 0, 0], out[:, 0, 1] = cosine, sine
    out[:, 1, 0], out[:, 1, 1] = -sine, cosine
    return out.reshape(2 * BOX, 2 * GRID).astype(ml_dtypes.bfloat16)


def y_table():
    cosine, sine = dft_tables()
    out = np.zeros((2, 32, 2, GRID), np.float32)
    out[0, :BOX, 0], out[0, :BOX, 1] = cosine, sine
    out[1, :BOX, 0], out[1, :BOX, 1] = -sine, cosine
    return out.reshape(64, 2 * GRID).astype(ml_dtypes.bfloat16)


def val_spread():
    out = np.zeros((NV, 2, 2, 2, 2, NV, NC), np.float32)
    for v in range(NV):
        for p in range(2):
            for i in range(2):
                out[v, p, i, i, p, v, :] = 1.0
    return out.reshape(8, 256).astype(ml_dtypes.bfloat16)


def cond_spread():
    out = np.zeros((2, 2, NC, 2, 2, NV, NC), np.float32)
    for p in range(2):
        for i in range(2):
            for c in range(NC):
                out[p, i, c, i, p, :, c] = 1.0
    return out.reshape(128, 256).astype(ml_dtypes.bfloat16)


def dot(left, right):
    return jnp.dot(left, right, preferred_element_type=jnp.float32)


def tables():
    out = np.zeros((128, 256), ml_dtypes.bfloat16)
    out[:64, : 2 * GRID] = y_table()
    out[64:112, : 2 * GRID] = z_table()
    out[112:120] = val_spread()
    return out


def spread_kernel(cond_ref, cs_ref, out_ref):
    out_ref[0] = dot(cond_ref[0, 0], cs_ref[...]).astype(jnp.bfloat16)


def spread_cond(cond):
    planes, points = cond.shape[1:3]
    chunk = points // 3
    return pl.pallas_call(
        spread_kernel,
        grid=(planes, 3),
        in_specs=[
            pl.BlockSpec((1, 1, chunk, 128), lambda a, g: (0, a, g, 0)),
            pl.BlockSpec((128, 256), lambda a, g: (0, 0)),
        ],
        out_specs=pl.BlockSpec((1, chunk, 256), lambda a, g: (a, g, 0)),
        out_shape=jax.ShapeDtypeStruct((planes, points, 256), jnp.bfloat16),
        compiler_params=pltpu.CompilerParams(vmem_limit_bytes=20 * 2**20),
        cost_estimate=pl.CostEstimate(
            flops=2_000_000_000, bytes_accessed=20_000_000, transcendentals=0
        ),
    )(cond, cond_spread())


def field_kernel(val_ref, cond_ref, table_ref, out_ref, zs_ref, pair_ref, y_ref):
    points = YCHUNK * GRID
    steps = GRID // YCHUNK
    ty = table_ref[:64, : 2 * GRID]
    tz = table_ref[64:112, : 2 * GRID]
    vs = table_ref[112:120, :]

    def pairs(slot):
        val = jnp.concatenate(
            [val_ref[v].astype(jnp.float32) for v in range(NV)], axis=0
        ).astype(jnp.bfloat16)
        spread = lax.dot_general(
            val, vs, (((0,), (0,)), ((), ())), preferred_element_type=jnp.float32
        )
        cond = cond_ref[0].astype(jnp.float32)
        val_re, val_im = spread[:, :128], spread[:, 128:]
        cond_re, cond_im = cond[:, :128], cond[:, 128:]
        pair_ref[slot, 0] = (val_re * cond_re + val_im * cond_im).astype(jnp.bfloat16)
        pair_ref[slot, 1] = (val_re * cond_im - val_im * cond_re).astype(jnp.bfloat16)

    def z_pass(step, slot):
        for y in range(0, YCHUNK, 2):
            rhs = jnp.concatenate(
                [
                    jnp.concatenate(
                        [pair_ref[slot, i, (y + u) * GRID : (y + u + 1) * GRID] for u in range(2)],
                        axis=1,
                    )
                    for i in range(2)
                ],
                axis=0,
            )
            z_out = dot(tz, rhs)
            for u in range(2):
                zs_ref[pl.ds(step * YCHUNK + y + u, 2 * BOX, stride=ZROW), :] = z_out[
                    :, u * 128 : (u + 1) * 128
                ]

    def y_pass():
        for fz in range(0, BOX, 2):
            rhs = jnp.concatenate(
                [
                    jnp.concatenate(
                        [
                            zs_ref[pl.ds(((fz + u) * 2 + i) * ZROW, GRID), :].astype(jnp.bfloat16)
                            for i in range(2)
                        ],
                        axis=0,
                    )
                    for u in range(2)
                ],
                axis=1,
            )
            y_out = dot(ty, rhs).astype(jnp.bfloat16)
            for u in range(2):
                for i in range(2):
                    y_ref[(fz + u) * 32 : (fz + u + 1) * 32, i * 128 : (i + 1) * 128] = y_out[
                        i * 32 : (i + 1) * 32, u * 128 : (u + 1) * 128
                    ]
        out_ref[0] = y_ref[...].T

    step = pl.program_id(1)

    @pl.when(step == 0)
    def _():
        pairs(0)

    @pl.when(step > 0)
    def _():
        z_pass(step - 1, (step - 1) % 2)
        pairs(step % 2)

    @pl.when(step == steps - 1)
    def _():
        z_pass(step, step % 2)
        y_pass()


def fields(val, cond, first):
    planes = val.shape[2] // (GRID * GRID)
    chunks = GRID // YCHUNK
    return pl.pallas_call(
        field_kernel,
        grid=(planes, chunks),
        in_specs=[
            pl.BlockSpec((NV, 4, YCHUNK * GRID), lambda a, g: (0, 0, a * chunks + g)),
            pl.BlockSpec((1, YCHUNK * GRID, 256), lambda a, g: (first + a, g, 0)),
            pl.BlockSpec((128, 256), lambda a, g: (0, 0)),
        ],
        out_specs=pl.BlockSpec((1, 256, COLS), lambda a, g: (a, 0, 0)),
        out_shape=jax.ShapeDtypeStruct((planes, 256, COLS), jnp.bfloat16),
        scratch_shapes=[
            pltpu.VMEM((2 * BOX * ZROW, 128), jnp.float32),
            pltpu.VMEM((2, 2, YCHUNK * GRID, 128), jnp.bfloat16),
            pltpu.VMEM((COLS, 256), jnp.bfloat16),
        ],
        compiler_params=pltpu.CompilerParams(vmem_limit_bytes=24 * 2**20),
        cost_estimate=pl.CostEstimate(
            flops=2_000_000_000, bytes_accessed=3_000_000, transcendentals=0
        ),
    )(val, cond, tables())


def x_phases(planes):
    angle = np.mod(
        np.arange(-BOX // 2 - 2, 32 - BOX // 2 - 2)[None, :] * np.arange(GRID)[:, None], GRID
    ).astype(np.float32) * np.float32(2.0 * math.pi / GRID)
    out = np.zeros((GRID // (2 * planes), 2, 8, 32), np.float32)
    out[:, 0, : 2 * planes] = np.cos(angle).reshape(-1, 2 * planes, 32)
    out[:, 1, : 2 * planes] = np.sin(angle).reshape(-1, 2 * planes, 32)
    return out.reshape(-1, 16, 32).astype(ml_dtypes.bfloat16)


def whole_div(value, by):
    return ((value.astype(jnp.float32) + 0.5) * (1.0 / by)).astype(jnp.int32)


def pick_kernel(first, away, umklapp_ref, sphere_ref, xt_ref, *refs):
    y_refs, out_ref = refs[:-1], refs[-1]
    place = lax.axis_index("fft")
    offset = umklapp_ref[lax.rem(lax.axis_index("ka") + 12, 16)]
    part = lax.rem(place // 8 + (1 if away else 0), 2)
    table = xt_ref[place]

    def tile(step, carry):
        index = jnp.concatenate(
            [
                sphere_ref[pl.ds((first + step * (PICK // HALF) + u) * 2 + part, 1), :]
                for u in range(PICK // HALF)
            ],
            axis=1,
        )
        x_freq = whole_div(index, BOX * BOX)
        plane = index - x_freq * (BOX * BOX)
        y_freq = whole_div(plane, BOX)
        column = (plane - y_freq * BOX) * 32 + y_freq
        spot = lax.broadcasted_iota(jnp.int32, (COLS, PICK), 0)
        chosen = jnp.where(column == spot, 1.0, 0.0).astype(jnp.bfloat16)
        freq = jnp.where(x_freq - offset + 2 == spot[:32], 1.0, 0.0).astype(jnp.bfloat16)
        phase = dot(table, freq)
        real = jnp.zeros((64, PICK), jnp.float32)
        imag = jnp.zeros((64, PICK), jnp.float32)
        a = 0
        for y_ref in y_refs:
            for plane_at in range(y_ref.shape[0]):
                got = dot(y_ref[plane_at], chosen)
                for p in range(2):
                    cosine = phase[a * 2 + p : a * 2 + p + 1]
                    sine = phase[8 + a * 2 + p : 9 + a * 2 + p]
                    got_re = got[p * 64 : (p + 1) * 64]
                    got_im = got[128 + p * 64 : 128 + (p + 1) * 64]
                    real = real + cosine * got_re + sine * got_im
                    imag = imag + cosine * got_im - sine * got_re
                a += 1
        scale = 1.0 / (GRID * math.sqrt(GRID))
        both = (jnp.concatenate([real, imag], axis=0) * scale).astype(jnp.bfloat16)
        out_ref[pl.ds(pl.multiple_of(step * PICK, PICK), PICK), :] = both.T
        return carry

    lax.fori_loop(0, out_ref.shape[0] // PICK, tile, 0, unroll=4)


def pick(first, count, away, umklapp, sphere, planes):
    vmem = pl.BlockSpec(memory_space=pltpu.VMEM)
    return pl.pallas_call(
        functools.partial(pick_kernel, first, away),
        in_specs=[pl.BlockSpec(memory_space=pltpu.SMEM)] + [vmem] * (2 + len(planes)),
        out_specs=vmem,
        out_shape=jax.ShapeDtypeStruct((count * HALF, 128), jnp.bfloat16),
        compiler_params=pltpu.CompilerParams(vmem_limit_bytes=24 * 2**20),
        cost_estimate=pl.CostEstimate(
            flops=100_000_000, bytes_accessed=500_000, transcendentals=0
        ),
    )(umklapp, sphere, x_phases(3), *planes)


def chi_kernel(
    e_val_ref, occ_val_ref, e_cond_ref, occ_cond_ref, own_ref, other_ref, near_ref, far_ref,
    out_ref, wa_ref,
):
    lane = lax.broadcasted_iota(jnp.int32, (1, 128), 1)
    sign = jnp.where(lane < 64, 1.0, -1.0)
    band = (lane // NC) % NV == 0
    e_cond = jnp.concatenate([e_cond_ref[...]] * 4, axis=1)
    occ_cond = jnp.concatenate([occ_cond_ref[...].astype(jnp.float32)] * 4, axis=1)
    for row in range(own_ref.shape[0]):
        k = (row + 12) % 16
        e_val = jnp.where(band, e_val_ref[0, k], e_val_ref[1, k])
        occ_val = jnp.where(band, occ_val_ref[0, k], occ_val_ref[1, k]).astype(jnp.float32)
        weight = (occ_val - occ_cond[row : row + 1]) / (
            (e_val - e_cond[row : row + 1]) * (16 * NV)
        )
        for h, ref in enumerate((own_ref, other_ref)):
            weighted = ref[row].astype(jnp.float32) * weight
            weighted = weighted.astype(jnp.bfloat16).astype(jnp.float32)
            wa_ref[row, (2 * h) * HALF : (2 * h + 1) * HALF] = weighted.astype(jnp.bfloat16)
            wa_ref[row, (2 * h + 1) * HALF : (2 * h + 2) * HALF] = (
                pltpu.roll(weighted, 64, 1) * sign
            ).astype(jnp.bfloat16)
    at = lax.axis_index("ka")
    y, x, c = at // 8, lax.rem(at // 2, 4), lax.rem(at, 2)
    total = jnp.zeros((4 * HALF, ROWS), jnp.float32)
    for dc, ref in enumerate((near_ref, far_ref)):
        for s in range(4):
            rows = [
                lax.rem(y + dy, 2) * 8 + lax.rem(x + 4 - s, 4) * 2 + lax.rem(c + dc, 2)
                for dy in range(2)
            ]
            left = jnp.concatenate([wa_ref[r] for r in rows], axis=1)
            right = jnp.concatenate(
                [ref[(2 * s + u) * ROWS : (2 * s + u + 1) * ROWS, :] for u in range(2)], axis=1
            )
            total = total + lax.dot_general(
                left, right, (((1,), (1,)), ((), ())), preferred_element_type=jnp.float32
            )
    half = lax.axis_index("fft") // 8
    for h in range(2):
        start = pl.multiple_of(lax.rem(half + h, 2) * HALF, HALF)
        for i in range(2):
            out_ref[pl.ds(start, HALF), i, :] = total[(2 * h + i) * HALF : (2 * h + i + 1) * HALF]


def contract(e_val, occ_val, e_cond, occ_cond, own, other, near, far):
    smem = pl.BlockSpec(memory_space=pltpu.SMEM)
    vmem = pl.BlockSpec(memory_space=pltpu.VMEM)
    return pl.pallas_call(
        chi_kernel,
        in_specs=[smem, smem] + [vmem] * 6,
        out_specs=vmem,
        out_shape=jax.ShapeDtypeStruct((ROWS, 2, ROWS), jnp.float32),
        scratch_shapes=[pltpu.VMEM((16, 4 * HALF, 128), jnp.bfloat16)],
        compiler_params=pltpu.CompilerParams(vmem_limit_bytes=24 * 2**20),
        cost_estimate=pl.CostEstimate(
            flops=600_000_000, bytes_accessed=4_000_000, transcendentals=0
        ),
    )(e_val.T, occ_val.T, e_cond, occ_cond, own, other, near, far)


def ka_route(move):
    route = []
    for i in range(16):
        y, x, c = move(i // 8, (i // 2) % 4, i % 2)
        route.append((i, (y % 2) * 8 + (x % 4) * 2 + c % 2))
    return route


def fft_route(move):
    route = []
    for i in range(16):
        y, z = move(i // 8, i % 8)
        route.append((i, (y % 2) * 8 + z % 8))
    return route


def mesh_route(move):
    route = []
    for k in range(16):
        for f in range(16):
            to_k, to_f = move(k, f)
            route.append((k * 16 + f, to_k * 16 + to_f))
    return route


def shards(psi_val, psi_cond, e_val, e_cond, occ_val, occ_cond, umklapp, sphere):
    count_k = 16
    step_q = 4
    planes = psi_cond.shape[1]
    shift = [(i, (i + step_q) % count_k) for i in range(count_k)]
    val = lax.ppermute(psi_val, "ka", shift)[0]
    field = [fields(val, spread_cond(psi_cond), 0)]
    sphere = sphere.reshape(NG // HALF, HALF)
    swap = fft_route(lambda y, z: (y + 1, z))
    shares = []
    sent = [None, None]
    for i, at in enumerate((0, 8)):
        sent[i] = pick(at, 8, True, umklapp, sphere, field)
        sent[i], *field = lax.optimization_barrier((sent[i], *field))
    came = [lax.ppermute(part, "fft", swap) for part in sent]
    for i, at in enumerate((0, 8)):
        kept = pick(at, 8, False, umklapp, sphere, field)
        shares.append((kept.astype(jnp.float32) + came[i].astype(jnp.float32)).astype(jnp.bfloat16))
        shares[i], *field = lax.optimization_barrier((shares[i], *field))
    share = jnp.concatenate(shares)
    spread = lax.all_to_all(share.reshape(16, HALF, 128), "fft", 0, 0)
    rho = spread.reshape(2, 8, HALF, 128).astype(jnp.float32).sum(1).astype(jnp.bfloat16)
    rho = rho.reshape(ROWS, 128)
    own = lax.ppermute(rho, ("ka", "fft"), mesh_route(lambda k, f: (f, k)))
    across = lax.ppermute(rho, "ka", ka_route(lambda y, x, c: (y + 1, x, c)))
    block = jnp.concatenate([rho, across])
    own, block = lax.optimization_barrier((own, block))
    ring = [
        lax.ppermute(block, "ka", ka_route(lambda y, x, c, s=s: (y, x + s, c))) for s in (1, 2, 3)
    ]
    copies = jnp.broadcast_to(own.reshape(2, 1, HALF, 128), (2, 8, HALF, 128))
    mine = lax.all_to_all(copies.reshape(16, HALF, 128), "fft", 0, 0)
    near = jnp.concatenate([block] + ring)
    near, mine = lax.optimization_barrier((near, mine))
    other = lax.ppermute(mine, "fft", swap)
    far = lax.ppermute(near, "ka", ka_route(lambda y, x, c: (y, x, c + 1)))
    return contract(e_val, occ_val, e_cond, occ_cond, mine, other, near, far)


def solution(mesh):
    placed = (P("ka", None, None, "fft"), P("ka", "fft", None, None), P(), P(), P(), P(), P(), P())
    return jax.shard_map(
        shards, mesh=mesh, in_specs=placed, out_specs=P("ka", None, "fft"), check_vma=False
    )
```

```python
import functools
import math

import jax
import jax.numpy as jnp
import ml_dtypes
import numpy as np
from jax import lax
from jax.experimental import pallas as pl
from jax.experimental.pallas import tpu as pltpu
from jax.sharding import PartitionSpec as P

GRID = 96
BOX = 24
NG = 4096
NV = 2
NC = 32
COLS = 768
ROWS = 256
HALF = 128
YCHUNK = 48
ZROW = 104
PICK = 256


def dft_tables():
    turns = np.mod((np.arange(BOX) - BOX // 2)[:, None] * np.arange(GRID)[None, :], GRID)
    angle = turns.astype(np.float32) * np.float32(2.0 * math.pi / GRID)
    return np.cos(angle), np.sin(angle)


def z_table():
    cosine, sine = dft_tables()
    out = np.zeros((BOX, 2, 2, GRID), np.float32)
    out[:, 0, 0], out[:, 0, 1] = cosine, sine
    out[:, 1, 0], out[:, 1, 1] = -sine, cosine
    return out.reshape(2 * BOX, 2 * GRID).astype(ml_dtypes.bfloat16)


def y_table():
    cosine, sine = dft_tables()
    out = np.zeros((2, 32, 2, GRID), np.float32)
    out[0, :BOX, 0], out[0, :BOX, 1] = cosine, sine
    out[1, :BOX, 0], out[1, :BOX, 1] = -sine, cosine
    return out.reshape(64, 2 * GRID).astype(ml_dtypes.bfloat16)


def val_spread():
    out = np.zeros((NV, 2, 2, 2, 2, NV, NC), np.float32)
    for v in range(NV):
        for p in range(2):
            for i in range(2):
                out[v, p, i, i, p, v, :] = 1.0
    return out.reshape(8, 256).astype(ml_dtypes.bfloat16)


def cond_spread():
    out = np.zeros((2, 2, NC, 2, 2, NV, NC), np.float32)
    for p in range(2):
        for i in range(2):
            for c in range(NC):
                out[p, i, c, i, p, :, c] = 1.0
    return out.reshape(128, 256).astype(ml_dtypes.bfloat16)


def dot(left, right):
    return jnp.dot(left, right, preferred_element_type=jnp.float32)


def tables():
    out = np.zeros((128, 256), ml_dtypes.bfloat16)
    out[:64, : 2 * GRID] = y_table()
    out[64:112, : 2 * GRID] = z_table()
    out[112:120] = val_spread()
    return out


def spread_kernel(cond_ref, cs_ref, out_ref):
    out_ref[0] = dot(cond_ref[0, 0], cs_ref[...]).astype(jnp.bfloat16)


def spread_cond(cond):
    planes, points = cond.shape[1:3]
    chunk = points // 3
    return pl.pallas_call(
        spread_kernel,
        grid=(planes, 3),
        in_specs=[
            pl.BlockSpec((1, 1, chunk, 128), lambda a, g: (0, a, g, 0)),
            pl.BlockSpec((128, 256), lambda a, g: (0, 0)),
        ],
        out_specs=pl.BlockSpec((1, chunk, 256), lambda a, g: (a, g, 0)),
        out_shape=jax.ShapeDtypeStruct((planes, points, 256), jnp.bfloat16),
        compiler_params=pltpu.CompilerParams(vmem_limit_bytes=20 * 2**20),
        cost_estimate=pl.CostEstimate(
            flops=2_000_000_000, bytes_accessed=20_000_000, transcendentals=0
        ),
    )(cond, cond_spread())


def field_kernel(val_ref, cond_ref, table_ref, out_ref, zs_ref, pair_ref, y_ref):
    points = YCHUNK * GRID
    steps = GRID // YCHUNK
    ty = table_ref[:64, : 2 * GRID]
    tz = table_ref[64:112, : 2 * GRID]
    vs = table_ref[112:128, :]

    def pairs(slot):
        val = jnp.concatenate(
            [val_ref[v].astype(jnp.float32) for v in range(NV)]
            + [jnp.zeros((8, points), jnp.float32)],
            axis=0,
        ).astype(jnp.bfloat16)
        spread = lax.dot_general(
            val, vs, (((0,), (0,)), ((), ())), preferred_element_type=jnp.float32
        )
        cond = cond_ref[0].astype(jnp.float32)
        val_re, val_im = spread[:, :128], spread[:, 128:]
        cond_re, cond_im = cond[:, :128], cond[:, 128:]
        pair_ref[slot, 0] = (val_re * cond_re + val_im * cond_im).astype(jnp.bfloat16)
        pair_ref[slot, 1] = (val_re * cond_im - val_im * cond_re).astype(jnp.bfloat16)

    def z_pass(step, slot):
        for y in range(0, YCHUNK, 2):
            rhs = jnp.concatenate(
                [
                    jnp.concatenate(
                        [pair_ref[slot, i, (y + u) * GRID : (y + u + 1) * GRID] for u in range(2)],
                        axis=1,
                    )
                    for i in range(2)
                ],
                axis=0,
            )
            z_out = dot(tz, rhs)
            for u in range(2):
                zs_ref[pl.ds(step * YCHUNK + y + u, 2 * BOX, stride=ZROW), :] = z_out[
                    :, u * 128 : (u + 1) * 128
                ]

    def y_pass():
        for fz in range(0, BOX, 2):
            rhs = jnp.concatenate(
                [
                    jnp.concatenate(
                        [
                            zs_ref[pl.ds(((fz + u) * 2 + i) * ZROW, GRID), :].astype(jnp.bfloat16)
                            for i in range(2)
                        ],
                        axis=0,
                    )
                    for u in range(2)
                ],
                axis=1,
            )
            y_out = dot(ty, rhs).astype(jnp.bfloat16)
            for u in range(2):
                for i in range(2):
                    y_ref[(fz + u) * 32 : (fz + u + 1) * 32, i * 128 : (i + 1) * 128] = y_out[
                        i * 32 : (i + 1) * 32, u * 128 : (u + 1) * 128
                    ]
        out_ref[0] = y_ref[...].T

    step = pl.program_id(1)

    @pl.when(step == 0)
    def _():
        pairs(0)

    @pl.when(step > 0)
    def _():
        z_pass(step - 1, (step - 1) % 2)
        pairs(step % 2)

    @pl.when(step == steps - 1)
    def _():
        z_pass(step, step % 2)
        y_pass()


def fields(val, cond, first):
    planes = val.shape[2] // (GRID * GRID)
    chunks = GRID // YCHUNK
    return pl.pallas_call(
        field_kernel,
        grid=(planes, chunks),
        in_specs=[
            pl.BlockSpec((NV, 4, YCHUNK * GRID), lambda a, g: (0, 0, a * chunks + g)),
            pl.BlockSpec((1, YCHUNK * GRID, 256), lambda a, g: (first + a, g, 0)),
            pl.BlockSpec((128, 256), lambda a, g: (0, 0)),
        ],
        out_specs=pl.BlockSpec((1, 256, COLS), lambda a, g: (a, 0, 0)),
        out_shape=jax.ShapeDtypeStruct((planes, 256, COLS), jnp.bfloat16),
        scratch_shapes=[
            pltpu.VMEM((2 * BOX * ZROW, 128), jnp.float32),
            pltpu.VMEM((2, 2, YCHUNK * GRID, 128), jnp.bfloat16),
            pltpu.VMEM((COLS, 256), jnp.bfloat16),
        ],
        compiler_params=pltpu.CompilerParams(vmem_limit_bytes=24 * 2**20),
        cost_estimate=pl.CostEstimate(
            flops=2_000_000_000, bytes_accessed=3_000_000, transcendentals=0
        ),
    )(val, cond, tables())


def x_phases(planes):
    angle = np.mod(
        np.arange(-BOX // 2 - 2, 32 - BOX // 2 - 2)[None, :] * np.arange(GRID)[:, None], GRID
    ).astype(np.float32) * np.float32(2.0 * math.pi / GRID)
    out = np.zeros((GRID // (2 * planes), 2, 8, 32), np.float32)
    out[:, 0, : 2 * planes] = np.cos(angle).reshape(-1, 2 * planes, 32)
    out[:, 1, : 2 * planes] = np.sin(angle).reshape(-1, 2 * planes, 32)
    return out.reshape(-1, 16, 32).astype(ml_dtypes.bfloat16)


def whole_div(value, by):
    return ((value.astype(jnp.float32) + 0.5) * (1.0 / by)).astype(jnp.int32)


def pick_kernel(first, away, umklapp_ref, sphere_ref, xt_ref, *refs):
    y_refs, out_ref = refs[:-1], refs[-1]
    place = lax.axis_index("fft")
    offset = umklapp_ref[lax.rem(lax.axis_index("ka") + 12, 16)]
    part = lax.rem(place // 8 + (1 if away else 0), 2)
    table = xt_ref[place]

    def tile(step, carry):
        index = jnp.concatenate(
            [
                sphere_ref[pl.ds((first + step * (PICK // HALF) + u) * 2 + part, 1), :]
                for u in range(PICK // HALF)
            ],
            axis=1,
        )
        x_freq = whole_div(index, BOX * BOX)
        plane = index - x_freq * (BOX * BOX)
        y_freq = whole_div(plane, BOX)
        column = (plane - y_freq * BOX) * 32 + y_freq
        spot = lax.broadcasted_iota(jnp.int32, (COLS, PICK), 0)
        chosen = jnp.where(column == spot, 1.0, 0.0).astype(jnp.bfloat16)
        freq = jnp.where(x_freq - offset + 2 == spot[:32], 1.0, 0.0).astype(jnp.bfloat16)
        phase = dot(table, freq)
        real = jnp.zeros((64, PICK), jnp.float32)
        imag = jnp.zeros((64, PICK), jnp.float32)
        a = 0
        for y_ref in y_refs:
            for plane_at in range(y_ref.shape[0]):
                got = dot(y_ref[plane_at], chosen)
                for p in range(2):
                    cosine = phase[a * 2 + p : a * 2 + p + 1]
                    sine = phase[8 + a * 2 + p : 9 + a * 2 + p]
                    got_re = got[p * 64 : (p + 1) * 64]
                    got_im = got[128 + p * 64 : 128 + (p + 1) * 64]
                    real = real + cosine * got_re + sine * got_im
                    imag = imag + cosine * got_im - sine * got_re
                a += 1
        scale = 1.0 / (GRID * math.sqrt(GRID))
        both = (jnp.concatenate([real, imag], axis=0) * scale).astype(jnp.bfloat16)
        out_ref[pl.ds(pl.multiple_of(step * PICK, PICK), PICK), :] = both.T
        return carry

    lax.fori_loop(0, out_ref.shape[0] // PICK, tile, 0, unroll=4)


def pick(first, count, away, umklapp, sphere, planes):
    vmem = pl.BlockSpec(memory_space=pltpu.VMEM)
    return pl.pallas_call(
        functools.partial(pick_kernel, first, away),
        in_specs=[pl.BlockSpec(memory_space=pltpu.SMEM)] + [vmem] * (2 + len(planes)),
        out_specs=vmem,
        out_shape=jax.ShapeDtypeStruct((count * HALF, 128), jnp.bfloat16),
        compiler_params=pltpu.CompilerParams(vmem_limit_bytes=24 * 2**20),
        cost_estimate=pl.CostEstimate(
            flops=100_000_000, bytes_accessed=500_000, transcendentals=0
        ),
    )(umklapp, sphere, x_phases(3), *planes)


def chi_kernel(
    e_val_ref, occ_val_ref, e_cond_ref, occ_cond_ref, own_ref, other_ref, near_ref, far_ref,
    out_ref, wa_ref,
):
    lane = lax.broadcasted_iota(jnp.int32, (1, 128), 1)
    sign = jnp.where(lane < 64, 1.0, -1.0)
    band = (lane // NC) % NV == 0
    e_cond = jnp.concatenate([e_cond_ref[...]] * 4, axis=1)
    occ_cond = jnp.concatenate([occ_cond_ref[...].astype(jnp.float32)] * 4, axis=1)
    for row in range(own_ref.shape[0]):
        k = (row + 12) % 16
        e_val = jnp.where(band, e_val_ref[0, k], e_val_ref[1, k])
        occ_val = jnp.where(band, occ_val_ref[0, k], occ_val_ref[1, k]).astype(jnp.float32)
        weight = (occ_val - occ_cond[row : row + 1]) / (
            (e_val - e_cond[row : row + 1]) * (16 * NV)
        )
        for h, ref in enumerate((own_ref, other_ref)):
            weighted = ref[row].astype(jnp.float32) * weight
            weighted = weighted.astype(jnp.bfloat16).astype(jnp.float32)
            wa_ref[row, (2 * h) * HALF : (2 * h + 1) * HALF] = weighted.astype(jnp.bfloat16)
            wa_ref[row, (2 * h + 1) * HALF : (2 * h + 2) * HALF] = (
                pltpu.roll(weighted, 64, 1) * sign
            ).astype(jnp.bfloat16)
    at = lax.axis_index("ka")
    y, x, c = at // 8, lax.rem(at // 2, 4), lax.rem(at, 2)
    total = jnp.zeros((4 * HALF, ROWS), jnp.float32)
    for dc, ref in enumerate((near_ref, far_ref)):
        for s in range(4):
            rows = [
                lax.rem(y + dy, 2) * 8 + lax.rem(x + 4 - s, 4) * 2 + lax.rem(c + dc, 2)
                for dy in range(2)
            ]
            left = jnp.concatenate([wa_ref[r] for r in rows], axis=1)
            right = jnp.concatenate(
                [ref[(2 * s + u) * ROWS : (2 * s + u + 1) * ROWS, :] for u in range(2)], axis=1
            )
            total = total + lax.dot_general(
                left, right, (((1,), (1,)), ((), ())), preferred_element_type=jnp.float32
            )
    half = lax.axis_index("fft") // 8
    for h in range(2):
        start = pl.multiple_of(lax.rem(half + h, 2) * HALF, HALF)
        for i in range(2):
            out_ref[pl.ds(start, HALF), i, :] = total[(2 * h + i) * HALF : (2 * h + i + 1) * HALF]


def contract(e_val, occ_val, e_cond, occ_cond, own, other, near, far):
    smem = pl.BlockSpec(memory_space=pltpu.SMEM)
    vmem = pl.BlockSpec(memory_space=pltpu.VMEM)
    return pl.pallas_call(
        chi_kernel,
        in_specs=[smem, smem] + [vmem] * 6,
        out_specs=vmem,
        out_shape=jax.ShapeDtypeStruct((ROWS, 2, ROWS), jnp.float32),
        scratch_shapes=[pltpu.VMEM((16, 4 * HALF, 128), jnp.bfloat16)],
        compiler_params=pltpu.CompilerParams(vmem_limit_bytes=24 * 2**20),
        cost_estimate=pl.CostEstimate(
            flops=600_000_000, bytes_accessed=4_000_000, transcendentals=0
        ),
    )(e_val.T, occ_val.T, e_cond, occ_cond, own, other, near, far)


def ka_route(move):
    route = []
    for i in range(16):
        y, x, c = move(i // 8, (i // 2) % 4, i % 2)
        route.append((i, (y % 2) * 8 + (x % 4) * 2 + c % 2))
    return route


def fft_route(move):
    route = []
    for i in range(16):
        y, z = move(i // 8, i % 8)
        route.append((i, (y % 2) * 8 + z % 8))
    return route


def mesh_route(move):
    route = []
    for k in range(16):
        for f in range(16):
            to_k, to_f = move(k, f)
            route.append((k * 16 + f, to_k * 16 + to_f))
    return route


def shards(psi_val, psi_cond, e_val, e_cond, occ_val, occ_cond, umklapp, sphere):
    count_k = 16
    step_q = 4
    planes = psi_cond.shape[1]
    shift = [(i, (i + step_q) % count_k) for i in range(count_k)]
    val = lax.ppermute(psi_val, "ka", shift)[0]
    field = [fields(val, spread_cond(psi_cond), 0)]
    sphere = sphere.reshape(NG // HALF, HALF)
    swap = fft_route(lambda y, z: (y + 1, z))
    shares = []
    sent = [None, None]
    for i, at in enumerate((0, 8)):
        sent[i] = pick(at, 8, True, umklapp, sphere, field)
        sent[i], *field = lax.optimization_barrier((sent[i], *field))
    came = [lax.ppermute(part, "fft", swap) for part in sent]
    for i, at in enumerate((0, 8)):
        kept = pick(at, 8, False, umklapp, sphere, field)
        shares.append((kept.astype(jnp.float32) + came[i].astype(jnp.float32)).astype(jnp.bfloat16))
        shares[i], *field = lax.optimization_barrier((shares[i], *field))
    share = jnp.concatenate(shares)
    spread = lax.all_to_all(share.reshape(16, HALF, 128), "fft", 0, 0)
    rho = spread.reshape(2, 8, HALF, 128).astype(jnp.float32).sum(1).astype(jnp.bfloat16)
    rho = rho.reshape(ROWS, 128)
    own = lax.ppermute(rho, ("ka", "fft"), mesh_route(lambda k, f: (f, k)))
    across = lax.ppermute(rho, "ka", ka_route(lambda y, x, c: (y + 1, x, c)))
    block = jnp.concatenate([rho, across])
    own, block = lax.optimization_barrier((own, block))
    ring = [
        lax.ppermute(block, "ka", ka_route(lambda y, x, c, s=s: (y, x + s, c))) for s in (1, 2, 3)
    ]
    copies = jnp.broadcast_to(own.reshape(2, 1, HALF, 128), (2, 8, HALF, 128))
    mine = lax.all_to_all(copies.reshape(16, HALF, 128), "fft", 0, 0)
    near = jnp.concatenate([block] + ring)
    near, mine = lax.optimization_barrier((near, mine))
    other = lax.ppermute(mine, "fft", swap)
    far = lax.ppermute(near, "ka", ka_route(lambda y, x, c: (y, x, c + 1)))
    return contract(e_val, occ_val, e_cond, occ_cond, mine, other, near, far)


def solution(mesh):
    placed = (P("ka", None, None, "fft"), P("ka", "fft", None, None), P(), P(), P(), P(), P(), P())
    return jax.shard_map(
        shards, mesh=mesh, in_specs=placed, out_specs=P("ka", None, "fft"), check_vma=False
    )
```
